32 devices in a mesh: dp: 16 (over z, x, core), head: 2 (over y).
Axes of the slice: x: 2, y: 2, z: 4, core: 2. Of those that a mesh axis runs over, the one named last changes fastest.
Arguments:
- tokens: bfloat16 [4096, 1536], P(('dp', 'head')), may hold values from -6 to 6
- norm1_gain: float32 [1536], replicated, may hold values from 0.5 to 1.5
- w_query: bfloat16 [1536, 1536], P(None, 'head'), may hold values from -0.15625 to 0.15625
- w_key: bfloat16 [1536, 1536], P(None, 'head'), may hold values from -0.15625 to 0.15625
- w_value: bfloat16 [1536, 1536], P(None, 'head'), may hold values from -0.15625 to 0.15625
- w_path: bfloat16 [1536, 1536], P(None, 'head'), may hold values from -0.15625 to 0.15625
- w_beta: bfloat16 [1536, 12], P(None, 'head'), may hold values from -0.15625 to 0.15625
- conv_kernel: float32 [128, 12, 4], P(None, 'head'), may hold values from -4 to 4
- w_output: bfloat16 [1536, 1536], P(None, 'head'), may hold values from -0.625 to 0.625
- norm2_gain: float32 [1536], replicated, may hold values from 0.5 to 1.5
- w_gate: bfloat16 [1536, 4096], P(None, 'head'), may hold values from -0.15625 to 0.15625
- w_up: bfloat16 [1536, 4096], P(None, 'head'), may hold values from -0.15625 to 0.15625
- w_down: bfloat16 [1536, 4096], P(None, 'head'), may hold values from -0.09375 to 0.09375
- item_lengths: int32 [16], P('dp'), may hold values from 129 to 256, as said below
- cotangent: bfloat16 [4096, 1536], P(('dp', 'head')), may hold values from -6 to 6
Outputs:
- activations: bfloat16 [4096, 1536], P(('dp', 'head'))
- grad_tokens: float32 [4096, 1536], P(('dp', 'head'))
- grad_norm1_gain: float32 [1536], P(('dp', 'head'))
- grad_w_query: float32 [1536, 1536], P('dp', 'head')
- grad_w_key: float32 [1536, 1536], P('dp', 'head')
- grad_w_value: float32 [1536, 1536], P('dp', 'head')
- grad_w_path: float32 [1536, 1536], P('dp', 'head')
- grad_w_beta: float32 [1536, 12], P('dp', 'head')
- grad_conv_kernel: float32 [128, 12, 4], P('dp', 'head')
- grad_w_output: float32 [1536, 1536], P('dp', 'head')
- grad_norm2_gain: float32 [1536], P(('dp', 'head'))
- grad_w_gate: float32 [1536, 4096], P('dp', 'head')
- grad_w_up: float32 [1536, 4096], P('dp', 'head')
- grad_w_down: float32 [1536, 4096], P('dp', 'head')
The draws below stay inside these ranges and needn't reach their ends.
Inputs may be any that keep to these rules, and one draw needn't show every extreme that they name: `item_lengths`: each group's first item is longer than 128 slots; the slots after it form a second item; in every draw some group's first item fills all 256 slots.
All inputs are finite; a program needn't handle non-finite values.
Results may differ from the reference program's by a relative error of at most 0.012.
Values may be sent and summed in bfloat16 or wider, within the bound.
No kernel may reach another device: no remote copies, remote signals or barrier semaphores. Data moves between devices by JAX's collectives and lax.ppermute only.
A program may use at most 256 MiB of HBM per device.

```python
import jax
import jax.numpy as jnp
from jax import lax

D = 1536
HEADS = 12
DH = 128
FF = 4096
CONV = 4
BLOCK = 128
TOK_DEV = 128
GROUP_TOK = 256
GROUPS = 16
TOKENS = 4096


def draw_item_lengths(key, part):
    key = jax.random.fold_in(key, 7)
    first_key, second_key = jax.random.split(key)
    lengths = jax.random.randint(first_key, (GROUPS,), TOK_DEV + 1, GROUP_TOK + 1, dtype=jnp.int32)
    chosen = jax.random.randint(second_key, (), 0, GROUPS, dtype=jnp.int32)
    filled = jnp.full((GROUPS,), GROUP_TOK, jnp.int32)
    return jnp.where(jnp.arange(GROUPS, dtype=jnp.int32) == chosen, filled, lengths).astype(jnp.int32)


def raised(drawn, rng, source, target, shards_of, factor):
    def block_of(dim):
        return (jnp.arange(drawn.shape[dim]) // (drawn.shape[dim] // shards_of)).reshape((-1,) + (1,) * (drawn.ndim - 1 - dim))

    one_side = jax.random.permutation(rng, shards_of)[block_of(target)]
    other_side = (block_of(target) + shards_of // 2) % shards_of
    return jnp.where((block_of(source) == one_side) | (block_of(source) == other_side), factor * drawn, drawn)


def level_of(rng, shape, shards, smallest, largest):
    factor_of, own = 1.0, jax.random.fold_in(rng, 6)
    for position, blocks in shards:
        heights = jnp.exp(jax.random.uniform(jax.random.fold_in(own, position), (blocks,), jnp.float32, smallest / len(shards), largest / len(shards)))
        factor_of = factor_of * jnp.repeat(heights, shape[position] // blocks).reshape([-1 if axis == position else 1 for axis in range(len(shape))])
    return factor_of


def gaussian(key, dims, scale, most, cuts=(), kind=jnp.bfloat16):
    level = level_of(key, dims, cuts, -0.22, 0.18) if cuts else 1.0
    entries = jax.random.normal(key, dims, jnp.float32) * scale * level
    return jnp.minimum(jnp.maximum(entries, -most), most).astype(kind)


def noise_with(rng, dims, spread, bound, shards, heavy, held_as=jnp.bfloat16):
    drawn = spread * jax.random.normal(rng, dims, jnp.float32)
    if shards:
        drawn = drawn * level_of(rng, dims, shards, -0.22, 0.18)
    return jnp.clip(raised(drawn, jax.random.fold_in(rng, 3), *heavy), -bound, bound).astype(held_as)


def setup_inputs(seed: int = 0) -> dict:
    seeds = jax.random.split(jax.random.key(seed), 16)
    tokens = noise_with(seeds[0], (TOKENS, D), 1.0, 6.0, ((0, 32),), (0, 1, 32, 2.75))
    norm1_gain = jnp.clip(1.0 + 0.1 * jax.random.normal(seeds[1], (D,), jnp.float32), 0.5, 1.5)
    w_query = gaussian(seeds[2], (D, HEADS * DH), D ** -0.5, 0.15625, ((1, 2),))
    w_key = gaussian(seeds[3], (D, HEADS * DH), D ** -0.5, 0.15625, ((1, 2),))
    w_value = gaussian(seeds[4], (D, HEADS * DH), D ** -0.5, 0.15625, ((1, 2),))
    w_path = gaussian(seeds[5], (D, HEADS * DH), D ** -0.5, 0.15625, ((1, 2),))
    w_beta = gaussian(seeds[6], (D, HEADS), D ** -0.5, 0.15625, ((1, 2),))
    conv_kernel = gaussian(seeds[7], (DH, HEADS, CONV), 1.0, 4.0, ((1, 2),), jnp.float32)
    w_output = gaussian(seeds[8], (D, HEADS * DH), (HEADS * DH // 16) ** -0.5, 0.625, ((1, 2),))
    norm2_gain = jnp.clip(1.0 + 0.1 * jax.random.normal(seeds[9], (D,), jnp.float32), 0.5, 1.5)
    w_gate = gaussian(seeds[10], (D, FF), D ** -0.5, 0.15625, ((1, 2),))
    w_up = gaussian(seeds[11], (D, FF), D ** -0.5, 0.15625, ((1, 2),))
    w_down = gaussian(seeds[12], (D, FF), FF ** -0.5, 0.09375, ((1, 2),))
    item_lengths = draw_item_lengths(jax.random.fold_in(seeds[15], 71), 0)
    cotangent = noise_with(seeds[14], (TOKENS, D), 1.0, 6.0, ((0, 32),), (0, 1, 32, 2.75))
    return dict(tokens=tokens, norm1_gain=norm1_gain, w_query=w_query, w_key=w_key, w_value=w_value, w_path=w_path, w_beta=w_beta, conv_kernel=conv_kernel, w_output=w_output, norm2_gain=norm2_gain, w_gate=w_gate, w_up=w_up, w_down=w_down, item_lengths=item_lengths, cotangent=cotangent)


@jax.custom_vjp
def low(v):
    return lax.optimization_barrier(v.astype(jnp.bfloat16)).astype(jnp.float32)

@jax.custom_vjp
def low_back(v):
    return v

def low_keep(v):
    return (low(v), None)

def low_pass(kept, grad):
    return (grad,)

def back_keep(v):
    return (v, None)

def back_low(kept, grad):
    return (low(grad),)
low.defvjp(low_keep, low_pass)
low_back.defvjp(back_keep, back_low)
eps_norm = 1e-06
highest = lax.Precision.HIGHEST

def fdot(left, right):
    return jnp.dot(left.astype(jnp.float32), right.astype(jnp.float32), precision=highest, preferred_element_type=jnp.float32)

def rms_scale(values, gain):
    return values * lax.rsqrt(lax.optimization_barrier(jnp.mean(values * values, axis=-1, keepdims=True)) + eps_norm) * gain

def short_conv(path_raw, kernel, segment):
    length = path_raw.shape[0]
    total = path_raw * kernel[0]
    for offset in range(1, kernel.shape[0]):
        shifted = jnp.concatenate([jnp.zeros((offset, path_raw.shape[1]), path_raw.dtype), path_raw[:length - offset]], axis=0)
        seg_shifted = jnp.concatenate([jnp.full((offset,), -1, segment.dtype), segment[:length - offset]])
        keep = (seg_shifted == segment).astype(path_raw.dtype)
        total = total + shifted * kernel[offset] * keep[:, None]
    return total

def block_terms(query_block, key_block, dir_block, beta_block):
    width = query_block.shape[0]
    lower_strict = jnp.tril(jnp.ones((width, width), jnp.float32), -1)
    lower_full = jnp.tril(jnp.ones((width, width), jnp.float32))
    gram = fdot(dir_block, dir_block.T)
    system = jnp.eye(width, dtype=jnp.float32) + beta_block[:, None] * gram * lower_strict
    factors = jax.scipy.linalg.solve_triangular(system, jnp.diag(beta_block), lower=True)
    query_dirs = fdot(query_block, dir_block.T) * lower_full
    dir_keys = fdot(dir_block, key_block.T) * lower_strict
    left_part = fdot(query_dirs, factors)
    right_part = fdot(factors, dir_keys)
    inner = fdot(query_block, key_block.T) - fdot(left_part, dir_keys)
    moved_queries = query_block - fdot(left_part, dir_block)
    moved_keys = key_block - fdot(right_part.T, dir_block)
    transfer = jnp.eye(dir_block.shape[1], dtype=jnp.float32) - fdot(dir_block.T, fdot(factors, dir_block))
    return (moved_queries, moved_keys, transfer, inner)

def attend_head(queries, keys, values, directions, betas, segment):
    length = queries.shape[0]
    count = length // BLOCK
    scale = queries.shape[1] ** (-0.5)
    col_pos = jnp.arange(length, dtype=jnp.int32)

    def step(carried, index):
        start = (index * BLOCK).astype(jnp.int32)
        query_block = lax.dynamic_slice_in_dim(queries, start, BLOCK, 0)
        key_block = lax.dynamic_slice_in_dim(keys, start, BLOCK, 0)
        dir_block = lax.dynamic_slice_in_dim(directions, start, BLOCK, 0)
        beta_block = lax.dynamic_slice_in_dim(betas, start, BLOCK, 0)
        moved_queries, moved_keys, transfer, inner = block_terms(query_block, key_block, dir_block, beta_block)
        cross = fdot(moved_queries, carried.T)
        placed = lax.dynamic_update_slice_in_dim(jnp.zeros_like(cross), inner, start, 1)
        inside = col_pos // BLOCK == index
        scores = jnp.where(inside[None, :], placed, cross) * scale
        row_pos = start + jnp.arange(BLOCK, dtype=jnp.int32)
        row_seg = lax.dynamic_slice_in_dim(segment, start, BLOCK, 0)
        allowed = (col_pos[None, :] <= row_pos[:, None]) & (segment[None, :] == row_seg[:, None])
        scores = jnp.where(allowed, scores, -1e+30)
        top = lax.optimization_barrier(jnp.max(scores, axis=1, keepdims=True))
        expd = jnp.exp(scores - top)
        probs = expd / lax.optimization_barrier(jnp.sum(expd, axis=1, keepdims=True))
        output = fdot(probs, values)
        carried = lax.dynamic_update_slice_in_dim(fdot(carried, transfer.T), moved_keys, start, 0)
        return (carried, output)
    _, outputs = lax.scan(jax.checkpoint(step), jnp.zeros_like(keys), jnp.arange(count, dtype=jnp.int32))
    return outputs.reshape(length, queries.shape[1])

def mixer(queries, keys, values, path_raw, beta_logit, kernel, segment):
    length = queries.shape[0]
    heads = beta_logit.shape[1]
    convolved = short_conv(path_raw, kernel, segment).reshape(length, heads, -1)
    directions = convolved * lax.rsqrt(lax.optimization_barrier(jnp.sum(convolved * convolved, axis=-1, keepdims=True)) + eps_norm)
    betas = 2.0 * jax.nn.sigmoid(beta_logit)

    def to_heads(array):
        return jnp.transpose(array.reshape(length, heads, -1), (1, 0, 2))
    mixed = jax.vmap(attend_head, in_axes=(0, 0, 0, 0, 1, None))(to_heads(queries), to_heads(keys), to_heads(values), jnp.transpose(directions, (1, 0, 2)), betas, segment)
    return jnp.transpose(mixed, (1, 0, 2)).reshape(length, -1)

def forward(params, segments):
    inputs, gain1, w_q, w_k, w_v, w_p, w_b, kernel_full, w_o, gain2, w_g, w_u, w_d = params
    normed1 = low(rms_scale(inputs, gain1))
    queries = low(low_back(fdot(normed1, w_q)))
    keys = low(low_back(fdot(normed1, w_k)))
    values = low(low_back(fdot(normed1, w_v)))
    path_raw = low_back(fdot(normed1, w_p))
    beta_logit = low_back(fdot(normed1, w_b))
    kernel = jnp.transpose(kernel_full, (2, 1, 0)).reshape(kernel_full.shape[2], -1)

    def group_mix(items):
        return mixer(items[0], items[1], items[2], items[3], items[4], kernel, items[5])
    grouped = (queries.reshape(GROUPS, GROUP_TOK, -1), keys.reshape(GROUPS, GROUP_TOK, -1), values.reshape(GROUPS, GROUP_TOK, -1), path_raw.reshape(GROUPS, GROUP_TOK, -1), beta_logit.reshape(GROUPS, GROUP_TOK, -1), segments)
    mixed = low(lax.map(group_mix, grouped).reshape(TOKENS, -1))
    attn = low_back(fdot(mixed, w_o.T))
    resid = inputs + attn
    normed2 = low(rms_scale(resid, gain2))
    gate = low_back(fdot(normed2, w_g))
    upper = low_back(fdot(normed2, w_u))
    hidden = low(jax.nn.silu(gate) * upper)
    return resid + low_back(fdot(hidden, w_d.T))

def reference(tokens, norm1_gain, w_query, w_key, w_value, w_path, w_beta, conv_kernel, w_output, norm2_gain, w_gate, w_up, w_down, item_lengths, cotangent):
    positions = jnp.arange(GROUP_TOK, dtype=jnp.int32)
    segments = (positions[None, :] >= item_lengths.astype(jnp.int32)[:, None]).astype(jnp.int32)
    params = tuple((array.astype(jnp.float32) for array in (tokens, norm1_gain, w_query, w_key, w_value, w_path, w_beta, conv_kernel, w_output, norm2_gain, w_gate, w_up, w_down)))
    result, pullback = jax.vjp(lambda packed: forward(packed, segments), params)
    grads = pullback(cotangent.astype(jnp.float32))[0]
    return (result.astype(jnp.bfloat16), grads[0], grads[1], grads[2], grads[3], grads[4], grads[5], grads[6], grads[7], grads[8], grads[9], grads[10], grads[11], grads[12])
```

```python
import jax
import numpy as np
import jax.numpy as jnp
from jax import lax
from jax.experimental import pallas as pl
from jax.experimental.pallas import tpu as pltpu
from jax.sharding import PartitionSpec as P

f32 = jnp.float32
bf = jnp.bfloat16
DH = 128
HB = 3


eps_norm = 1e-06


def dot_trans(left, right):
    return lax.dot_general(
        left, right, (((1,), (1,)), ((), ())), preferred_element_type=jnp.float32
    )


def trans_dot(left, right):
    return lax.dot_general(
        left, right, (((0,), (0,)), ((), ())), preferred_element_type=jnp.float32
    )


def rms_scale(values, gain):
    return values * lax.rsqrt(jnp.mean(values * values, axis=-1, keepdims=True) + eps_norm) * gain


def mm(a, b, ca, cb):
    return lax.dot_general(a, b, (((ca,), (cb,)), ((), ())), preferred_element_type=f32)


def parts(a):
    high = a.astype(bf)
    return high, (a - high.astype(f32)).astype(bf)


def mm3(a, b, ca, cb):
    (ah, al), (bh, bl) = a, b
    return mm(ah, bh, ca, cb) + mm(ah, bl, ca, cb) + mm(al, bh, ca, cb)


def mm2(a, b, ca, cb):
    return mm(a, b[0], ca, cb) + mm(a, b[1], ca, cb)


def index(shape):
    return lax.broadcasted_iota(jnp.int32, shape, 0), lax.broadcasted_iota(jnp.int32, shape, 1)


def column(array, which):
    lane = lax.broadcasted_iota(jnp.int32, array.shape, 1)
    return jnp.sum(jnp.where(lane == which, array, 0.0), axis=1, keepdims=True)


def shift_down(a, s):
    return jnp.concatenate([jnp.zeros((s, a.shape[1]), a.dtype), a[: a.shape[0] - s]], axis=0)


def shift_up(a, s):
    return jnp.concatenate([a[s:], jnp.zeros((s, a.shape[1]), a.dtype)], axis=0)


def kept(shape, s, first):
    t = lax.broadcasted_iota(jnp.int32, shape, 0)
    return (t >= s) & ~((t >= first) & (t - s < first))


def directions(path, taps, first):
    total = path * taps[0:1]
    for s in range(1, taps.shape[0]):
        total = total + jnp.where(kept(path.shape, s, first), shift_down(path, s), 0.0) * taps[s : s + 1]
    r = lax.rsqrt(jnp.sum(total * total, axis=1, keepdims=True) + 1e-6)
    return total * r, r


def inverses(systems):
    size = systems[0].shape[0]
    i, j = index((size, size))
    solved = [jnp.where(i == j, 1.0, 0.0) - jnp.where(i // 2 == j // 2, a, 0.0) for a in systems]
    width = 2
    while width < size:
        inside = (i // (2 * width) == j // (2 * width)) & (i // width != j // width)
        offs = [parts(jnp.where(inside, a, 0.0)) for a in systems]
        lows = [parts(x) for x in solved]
        inner = [parts(mm3(o, x, 1, 0)) for o, x in zip(offs, lows)]
        solved = [x - mm3(l, y, 1, 0) for x, l, y in zip(solved, lows, inner)]
        width *= 2
    return solved


def forward_kernel(first_ref, q_ref, k_ref, v_ref, path_ref, logit_ref, taps_ref, o_ref, x_ref, m_ref, p_ref):
    first = first_ref[0]
    rows = q_ref.shape[0]
    half = rows // 2
    base = pl.program_id(0) * HB
    heads = range(HB)
    cols = [slice(h * DH, (h + 1) * DH) for h in heads]
    i, j = index((rows, rows))
    q = [q_ref[:, c] for c in cols]
    k = [k_ref[:, c] for c in cols]
    w = [parts(directions(path_ref[:, c], taps_ref[:, c], first)[0]) for c in cols]
    logits = logit_ref[...]
    beta = [2.0 * jax.nn.sigmoid(column(logits, base + h)) for h in heads]
    system = [jnp.where(i > j, beta[h] * mm3(w[h], w[h], 1, 1), 0.0) for h in heads]
    corners = inverses([s[:half, :half] for s in system] + [s[half:, half:] for s in system])
    corners = [parts(x) for x in corners]
    low = [parts(mm3(parts(system[h][half:, :half]), corners[h], 1, 0)) for h in heads]
    low = [parts(-mm3(corners[HB + h], low[h], 1, 0)) for h in heads]
    zero = jnp.zeros((half, half), bf)
    x = [
        tuple(
            jnp.concatenate(
                [
                    jnp.concatenate([corners[h][n], zero], axis=1),
                    jnp.concatenate([low[h][n], corners[HB + h][n]], axis=1),
                ],
                axis=0,
            )
            for n in range(2)
        )
        for h in heads
    ]
    qw = [parts(jnp.where(i >= j, mm2(q[h], w[h], 1, 1), 0.0)) for h in heads]
    wk = [mm(w[h][0], k[h], 1, 1) + mm(w[h][1], k[h], 1, 1) for h in heads]
    wk = [parts(jnp.where(i > j, beta[h] * wk[h], 0.0)) for h in heads]
    m = [parts(mm3(qw[h], x[h], 1, 0)) for h in heads]
    s = [mm(q[h], k[h], 1, 1) - mm3(m[h], wk[h], 1, 0) for h in heads]
    allowed = (i >= j) & ((i < first) | (j >= first))
    s = [jnp.where(allowed, a * DH**-0.5, -1e30) for a in s]
    e = [jnp.exp(a - jnp.max(a, axis=1, keepdims=True)) for a in s]
    p = [(a / jnp.sum(a, axis=1, keepdims=True)).astype(bf) for a in e]
    for h in heads:
        o_ref[:, cols[h]] = mm(p[h], v_ref[:, cols[h]], 1, 0).astype(bf)
        x_ref[h] = x[h][0]
        m_ref[h] = m[h][0]
        p_ref[h] = p[h]


def backward_kernel(
    first_ref, q_ref, k_ref, v_ref, path_ref, logit_ref, taps_ref, x_ref, m_ref, p_ref, do_ref,
    dq_ref, dk_ref, dv_ref, dpath_ref, dlogit_ref, dtaps_ref,
):
    first = first_ref[0]
    rows = q_ref.shape[0]
    base = pl.program_id(0) * HB
    heads = range(HB)
    cols = [slice(h * DH, (h + 1) * DH) for h in heads]
    i, j = index((rows, rows))
    allowed = (i >= j) & ((i < first) | (j >= first))
    q = [q_ref[:, c] for c in cols]
    k = [k_ref[:, c] for c in cols]
    do = [do_ref[:, c].astype(bf) for c in cols]
    path = [path_ref[:, c] for c in cols]
    dirs = [directions(path[h], taps_ref[:, cols[h]], first) for h in heads]
    w = [d[0] for d in dirs]
    wb = [a.astype(bf) for a in w]
    logits = logit_ref[...]
    beta = [2.0 * jax.nn.sigmoid(column(logits, base + h)) for h in heads]
    p = [p_ref[h] for h in heads]
    x = [x_ref[h] for h in heads]
    m = [m_ref[h] for h in heads]
    dp = [mm(do[h], v_ref[:, cols[h]], 1, 1) for h in heads]
    for h in heads:
        dv_ref[:, cols[h]] = mm(p[h], do[h], 0, 0).astype(bf)
    p = [a.astype(f32) for a in p]
    sums = [jnp.sum(dp[h] * p[h], axis=1, keepdims=True) for h in heads]
    ds = [jnp.where(allowed, p[h] * (dp[h] - sums[h]) * DH**-0.5, 0.0).astype(bf) for h in heads]
    wk = [jnp.where(i > j, mm(wb[h], k[h], 1, 1), 0.0) for h in heads]
    gram = [mm(wb[h], wb[h], 1, 1) for h in heads]
    dm = [(-mm(ds[h], (beta[h] * wk[h]).astype(bf), 1, 1)).astype(bf) for h in heads]
    dwk = [jnp.where(i > j, -mm(m[h], ds[h], 0, 0), 0.0) for h in heads]
    z = [mm(dm[h], x[h], 1, 1) for h in heads]
    dbeta = [jnp.sum(dwk[h] * wk[h], axis=1, keepdims=True) for h in heads]
    dwk = [(beta[h] * dwk[h]).astype(bf) for h in heads]
    da = [jnp.where(i > j, -mm(m[h], z[h].astype(bf), 0, 0), 0.0) for h in heads]
    dqw = [jnp.where(i >= j, z[h], 0.0).astype(bf) for h in heads]
    dbeta = [dbeta[h] + jnp.sum(da[h] * gram[h], axis=1, keepdims=True) for h in heads]
    dg = [(beta[h] * da[h]).astype(bf) for h in heads]
    dw = [mm(dg[h], wb[h], 1, 0) + mm(dg[h], wb[h], 0, 0) + mm(dqw[h], q[h], 0, 0) + mm(dwk[h], k[h], 1, 0) for h in heads]
    for h in heads:
        dq_ref[:, cols[h]] = (mm(ds[h], k[h], 1, 0) + mm(dqw[h], wb[h], 1, 0)).astype(bf)
        dk_ref[:, cols[h]] = (mm(ds[h], q[h], 0, 0) + mm(dwk[h], wb[h], 0, 0)).astype(bf)
    lane = lax.broadcasted_iota(jnp.int32, logits.shape, 1)
    out = jnp.zeros_like(logits)
    for h in heads:
        out = out + jnp.where(lane == base + h, dbeta[h] * (beta[h] * (1.0 - 0.5 * beta[h])), 0.0)
        r = dirs[h][1]
        dc = r * (dw[h] - w[h] * jnp.sum(w[h] * dw[h], axis=1, keepdims=True))
        taps = taps_ref[:, cols[h]]
        dpath = dc * taps[0:1]
        dtaps = [jnp.sum(dc * path[h], axis=0, keepdims=True)]
        for s in range(1, taps.shape[0]):
            up = shift_up(jnp.where(kept(dc.shape, s, first), dc, 0.0), s)
            dpath = dpath + up * taps[s : s + 1]
            dtaps.append(jnp.sum(up * path[h], axis=0, keepdims=True))
        dpath_ref[:, cols[h]] = dpath.astype(bf)
        dtaps_ref[:, cols[h]] = jnp.concatenate(dtaps, axis=0)

    @pl.when(pl.program_id(0) == 0)
    def _():
        dlogit_ref[...] = out

    @pl.when(pl.program_id(0) > 0)
    def _():
        dlogit_ref[...] += out


VM = 60 * 1024 * 1024


def specs(rows, ntaps, nh):
    wide = pl.BlockSpec((rows, HB * DH), lambda n: (0, n))
    square = pl.BlockSpec((HB, rows, rows), lambda n: (n, 0, 0))
    logit = pl.BlockSpec((rows, nh), lambda n: (0, 0))
    taps = pl.BlockSpec((ntaps, HB * DH), lambda n: (0, n))
    smem = pl.BlockSpec(memory_space=pltpu.SMEM)
    return wide, square, logit, taps, smem


def mix_forward(first, q, k, v, path, logit, taps):
    rows, width = q.shape
    nh = width // DH
    wide, square, lg, tp, sm = specs(rows, taps.shape[0], nh)
    sq = jax.ShapeDtypeStruct((nh, rows, rows), bf)
    return pl.pallas_call(
        forward_kernel,
        grid=(nh // HB,),
        in_specs=[sm, wide, wide, wide, wide, lg, tp],
        out_specs=[wide, square, square, square],
        out_shape=[jax.ShapeDtypeStruct((rows, width), bf), sq, sq, sq],
        compiler_params=pltpu.CompilerParams(vmem_limit_bytes=VM),
        cost_estimate=pl.CostEstimate(flops=10 * 10**9, bytes_accessed=6 * 10**6, transcendentals=0),
        name="mix_forward",
    )(first, q, k, v, path, logit, taps)


def mix_backward(first, q, k, v, path, logit, taps, x, m, p, do):
    rows, width = q.shape
    nh = width // DH
    wide, square, lg, tp, sm = specs(rows, taps.shape[0], nh)
    low = jax.ShapeDtypeStruct((rows, width), bf)
    return pl.pallas_call(
        backward_kernel,
        grid=(nh // HB,),
        in_specs=[sm, wide, wide, wide, wide, lg, tp, square, square, square, wide],
        out_specs=[wide, wide, wide, wide, lg, tp],
        out_shape=[low, low, low, low, jax.ShapeDtypeStruct((rows, nh), f32), jax.ShapeDtypeStruct(taps.shape, f32)],
        compiler_params=pltpu.CompilerParams(vmem_limit_bytes=VM),
        cost_estimate=pl.CostEstimate(flops=10 * 10**9, bytes_accessed=6 * 10**6, transcendentals=0),
        name="mix_backward",
    )(first, q, k, v, path, logit, taps, x, m, p, do)


def per_device(
    tokens,
    norm1_gain,
    w_query,
    w_key,
    w_value,
    w_path,
    w_beta,
    conv_kernel,
    w_output,
    norm2_gain,
    w_gate,
    w_up,
    w_down,
    item_lengths,
    cotangent,
):
    local_rows = tokens.shape[0]
    group_rows = local_rows * lax.axis_size("head")
    inputs = tokens.astype(jnp.float32)
    normed1, norm1_back = jax.vjp(rms_scale, inputs, norm1_gain)
    rows_one = lax.all_gather(normed1.astype(jnp.bfloat16), "head", axis=0, tiled=True)

    def project(weight):
        return jnp.dot(rows_one, weight, preferred_element_type=jnp.float32)

    queries = project(w_query).astype(jnp.bfloat16)
    keys = project(w_key).astype(jnp.bfloat16)
    values = project(w_value).astype(jnp.bfloat16)
    path_raw = project(w_path)
    beta_logit = project(w_beta)
    kernel = jnp.transpose(conv_kernel, (2, 1, 0)).reshape(conv_kernel.shape[2], -1)

    mixed_low, solved, moved, probs = mix_forward(
        item_lengths, queries, keys, values, path_raw, beta_logit, kernel
    )
    attn_rows = lax.psum_scatter(
        dot_trans(mixed_low, w_output), "head", scatter_dimension=0, tiled=True
    )
    resid = inputs + attn_rows
    normed2, norm2_back = jax.vjp(rms_scale, resid, norm2_gain)
    rows_two = lax.all_gather(normed2.astype(jnp.bfloat16), "head", axis=0, tiled=True)
    gate = jnp.dot(rows_two, w_gate, preferred_element_type=jnp.float32)
    upper = jnp.dot(rows_two, w_up, preferred_element_type=jnp.float32)
    sigma = jax.nn.sigmoid(gate)
    activated = gate * sigma
    hidden_low = (activated * upper).astype(jnp.bfloat16)
    ffn_part = lax.psum_scatter(
        dot_trans(hidden_low, w_down).astype(jnp.bfloat16), "head", scatter_dimension=0, tiled=True
    ).astype(jnp.float32)
    activations = (resid + ffn_part).astype(jnp.bfloat16)
    grad_rows = lax.all_gather(cotangent, "head", axis=0, tiled=True)
    grad_hidden = jnp.dot(grad_rows, w_down, preferred_element_type=jnp.float32)
    grad_w_down = trans_dot(grad_rows, hidden_low)
    slope = sigma * (1.0 + gate * (1.0 - sigma))
    grad_gate = (grad_hidden * upper * slope).astype(jnp.bfloat16)
    grad_upper = (grad_hidden * activated).astype(jnp.bfloat16)
    grad_w_gate = trans_dot(rows_two, grad_gate)
    grad_w_up = trans_dot(rows_two, grad_upper)
    grad_normed2 = lax.psum_scatter(
        dot_trans(grad_gate, w_gate) + dot_trans(grad_upper, w_up),
        "head",
        scatter_dimension=0,
        tiled=True,
    )
    grad_resid_norm, grad_gain2 = norm2_back(grad_normed2)
    grad_resid = cotangent.astype(jnp.float32) + grad_resid_norm
    branch_rows = lax.all_gather(grad_resid.astype(jnp.bfloat16), "head", axis=0, tiled=True)
    grad_mixed = jnp.dot(branch_rows, w_output, preferred_element_type=jnp.float32)
    grad_w_output = trans_dot(branch_rows, mixed_low)
    query_low, key_low, value_low, path_low, grad_logit, grad_kernel = mix_backward(
        item_lengths, queries, keys, values, path_raw, beta_logit, kernel, solved, moved, probs, grad_mixed
    )
    logit_low = grad_logit.astype(jnp.bfloat16)
    grad_w_query = trans_dot(rows_one, query_low)
    grad_w_key = trans_dot(rows_one, key_low)
    grad_w_value = trans_dot(rows_one, value_low)
    grad_w_path = trans_dot(rows_one, path_low)
    grad_w_beta = trans_dot(rows_one, logit_low)
    grad_conv = jnp.transpose(
        grad_kernel.reshape(conv_kernel.shape[2], conv_kernel.shape[1], conv_kernel.shape[0]),
        (2, 1, 0),
    )
    total = dot_trans(query_low, w_query)
    total = total + dot_trans(key_low, w_key)
    total = total + dot_trans(value_low, w_value)
    total = total + dot_trans(path_low, w_path)
    grad_normed1 = lax.psum_scatter(
        (total + dot_trans(logit_low, w_beta)).astype(jnp.bfloat16),
        "head",
        scatter_dimension=0,
        tiled=True,
    ).astype(jnp.float32)
    grad_inputs_norm, grad_gain1 = norm1_back(grad_normed1)
    grad_tokens = grad_resid + grad_inputs_norm
    grad_gain1, grad_gain2 = (
        lax.psum_scatter(grad_gain1, ("dp", "head"), scatter_dimension=0, tiled=True),
        lax.psum_scatter(grad_gain2, ("dp", "head"), scatter_dimension=0, tiled=True),
    )
    def scatter(parts, dtype):
        joined = jnp.concatenate([part.astype(dtype) for part in parts], axis=1)
        joined = lax.psum_scatter(joined, "dp", scatter_dimension=0, tiled=True).astype(jnp.float32)
        return jnp.split(joined, np.cumsum([part.shape[1] for part in parts])[:-1], axis=1)

    grad_w_gate, grad_w_up, grad_w_down, grad_w_output = scatter(
        (grad_w_gate, grad_w_up, grad_w_down, grad_w_output), jnp.bfloat16
    )
    grad_w_query, grad_w_key, grad_w_value, grad_w_path = scatter(
        (grad_w_query, grad_w_key, grad_w_value, grad_w_path), jnp.bfloat16
    )
    shards = lax.axis_size("dp")
    conv_flat = grad_conv.reshape(shards, -1)
    grad_w_beta, conv_flat = scatter(
        (grad_w_beta.reshape(shards, -1), conv_flat), jnp.float32
    )
    grad_w_beta = grad_w_beta.reshape(-1, w_beta.shape[1])
    grad_conv = conv_flat.reshape((-1,) + conv_kernel.shape[1:])
    return (
        activations,
        grad_tokens,
        grad_gain1,
        grad_w_query,
        grad_w_key,
        grad_w_value,
        grad_w_path,
        grad_w_beta,
        grad_conv,
        grad_w_output,
        grad_gain2,
        grad_w_gate,
        grad_w_up,
        grad_w_down,
    )


def solution(mesh):
    in_specs = (
        P(("dp", "head"), None),
        P(),
        P(None, "head"),
        P(None, "head"),
        P(None, "head"),
        P(None, "head"),
        P(None, "head"),
        P(None, "head", None),
        P(None, "head"),
        P(),
        P(None, "head"),
        P(None, "head"),
        P(None, "head"),
        P("dp"),
        P(("dp", "head"), None),
    )
    out_specs = (
        P(("dp", "head"), None),
        P(("dp", "head"), None),
        P(("dp", "head")),
        P("dp", "head"),
        P("dp", "head"),
        P("dp", "head"),
        P("dp", "head"),
        P("dp", "head"),
        P("dp", "head", None),
        P("dp", "head"),
        P(("dp", "head")),
        P("dp", "head"),
        P("dp", "head"),
        P("dp", "head"),
    )
    return jax.shard_map(
        per_device, mesh=mesh, in_specs=in_specs, out_specs=out_specs, check_vma=False
    )
```

```python
import jax
import jax.numpy as jnp
from jax import lax
from jax.experimental import pallas as pl
from jax.experimental.pallas import tpu as pltpu
from jax.sharding import PartitionSpec as P

f32 = jnp.float32
bf = jnp.bfloat16
DH = 128
HB = 3


def mm(a, b, ca, cb):
    return lax.dot_general(a, b, (((ca,), (cb,)), ((), ())), preferred_element_type=f32)


def parts(a):
    high = a.astype(bf)
    return high, (a - high.astype(f32)).astype(bf)


def mm3(a, b, ca, cb):
    (ah, al), (bh, bl) = a, b
    return mm(ah, bh, ca, cb) + mm(ah, bl, ca, cb) + mm(al, bh, ca, cb)


def mm2(a, b, ca, cb):
    return mm(a, b[0], ca, cb) + mm(a, b[1], ca, cb)


def index(shape):
    return lax.broadcasted_iota(jnp.int32, shape, 0), lax.broadcasted_iota(jnp.int32, shape, 1)


def column(array, which):
    lane = lax.broadcasted_iota(jnp.int32, array.shape, 1)
    return jnp.sum(jnp.where(lane == which, array, 0.0), axis=1, keepdims=True)


def shift_down(a, s):
    return jnp.concatenate([jnp.zeros((s, a.shape[1]), a.dtype), a[: a.shape[0] - s]], axis=0)


def shift_up(a, s):
    return jnp.concatenate([a[s:], jnp.zeros((s, a.shape[1]), a.dtype)], axis=0)


def kept(shape, s, first):
    t = lax.broadcasted_iota(jnp.int32, shape, 0)
    return (t >= s) & ~((t >= first) & (t - s < first))


def directions(path, taps, first):
    total = path * taps[0:1]
    for s in range(1, taps.shape[0]):
        total = total + jnp.where(kept(path.shape, s, first), shift_down(path, s), 0.0) * taps[s : s + 1]
    r = lax.rsqrt(jnp.sum(total * total, axis=1, keepdims=True) + 1e-6)
    return total * r, r


def inverses(systems):
    size = systems[0].shape[0]
    i, j = index((size, size))
    solved = [jnp.where(i == j, 1.0, 0.0) - jnp.where(i // 2 == j // 2, a, 0.0) for a in systems]
    width = 2
    while width < size:
        inside = (i // (2 * width) == j // (2 * width)) & (i // width != j // width)
        offs = [parts(jnp.where(inside, a, 0.0)) for a in systems]
        lows = [parts(x) for x in solved]
        inner = [parts(mm3(o, x, 1, 0)) for o, x in zip(offs, lows)]
        solved = [x - mm3(l, y, 1, 0) for x, l, y in zip(solved, lows, inner)]
        width *= 2
    return solved


def forward_kernel(first_ref, q_ref, k_ref, v_ref, path_ref, logit_ref, taps_ref, o_ref, x_ref, m_ref, p_ref):
    first = first_ref[0]
    rows = q_ref.shape[0]
    half = rows // 2
    base = pl.program_id(0) * HB
    heads = range(HB)
    cols = [slice(h * DH, (h + 1) * DH) for h in heads]
    i, j = index((rows, rows))
    q = [q_ref[:, c] for c in cols]
    k = [k_ref[:, c] for c in cols]
    w = [parts(directions(path_ref[:, c], taps_ref[:, c], first)[0]) for c in cols]
    logits = logit_ref[...]
    beta = [2.0 * jax.nn.sigmoid(column(logits, base + h)) for h in heads]
    system = [jnp.where(i > j, beta[h] * mm3(w[h], w[h], 1, 1), 0.0) for h in heads]
    corners = inverses([s[:half, :half] for s in system] + [s[half:, half:] for s in system])
    corners = [parts(x) for x in corners]
    low = [parts(mm3(parts(system[h][half:, :half]), corners[h], 1, 0)) for h in heads]
    low = [parts(-mm3(corners[HB + h], low[h], 1, 0)) for h in heads]
    zero = jnp.zeros((half, half), bf)
    x = [
        tuple(
            jnp.concatenate(
                [
                    jnp.concatenate([corners[h][n], zero], axis=1),
                    jnp.concatenate([low[h][n], corners[HB + h][n]], axis=1),
                ],
                axis=0,
            )
            for n in range(2)
        )
        for h in heads
    ]
    qw = [parts(jnp.where(i >= j, mm2(q[h], w[h], 1, 1), 0.0)) for h in heads]
    wk = [mm(w[h][0], k[h], 1, 1) + mm(w[h][1], k[h], 1, 1) for h in heads]
    wk = [parts(jnp.where(i > j, beta[h] * wk[h], 0.0)) for h in heads]
    m = [parts(mm3(qw[h], x[h], 1, 0)) for h in heads]
    s = [mm(q[h], k[h], 1, 1) - mm3(m[h], wk[h], 1, 0) for h in heads]
    allowed = (i >= j) & ((i < first) | (j >= first))
    s = [jnp.where(allowed, a * DH**-0.5, -1e30) for a in s]
    e = [jnp.exp(a - jnp.max(a, axis=1, keepdims=True)) for a in s]
    p = [(a / jnp.sum(a, axis=1, keepdims=True)).astype(bf) for a in e]
    for h in heads:
        o_ref[:, cols[h]] = mm(p[h], v_ref[:, cols[h]], 1, 0).astype(bf)
        x_ref[h] = x[h][0]
        m_ref[h] = m[h][0]
        p_ref[h] = p[h]


def backward_kernel(
    first_ref, q_ref, k_ref, v_ref, path_ref, logit_ref, taps_ref, x_ref, m_ref, p_ref, do_ref,
    dq_ref, dk_ref, dv_ref, dpath_ref, dlogit_ref, dtaps_ref,
):
    first = first_ref[0]
    rows = q_ref.shape[0]
    base = pl.program_id(0) * HB
    heads = range(HB)
    cols = [slice(h * DH, (h + 1) * DH) for h in heads]
    i, j = index((rows, rows))
    allowed = (i >= j) & ((i < first) | (j >= first))
    q = [q_ref[:, c] for c in cols]
    k = [k_ref[:, c] for c in cols]
    do = [do_ref[:, c].astype(bf) for c in cols]
    path = [path_ref[:, c] for c in cols]
    dirs = [directions(path[h], taps_ref[:, cols[h]], first) for h in heads]
    w = [d[0] for d in dirs]
    wb = [a.astype(bf) for a in w]
    logits = logit_ref[...]
    beta = [2.0 * jax.nn.sigmoid(column(logits, base + h)) for h in heads]
    p = [p_ref[h] for h in heads]
    x = [x_ref[h] for h in heads]
    m = [m_ref[h] for h in heads]
    dp = [mm(do[h], v_ref[:, cols[h]], 1, 1) for h in heads]
    for h in heads:
        dv_ref[:, cols[h]] = mm(p[h], do[h], 0, 0).astype(bf)
    p = [a.astype(f32) for a in p]
    sums = [jnp.sum(dp[h] * p[h], axis=1, keepdims=True) for h in heads]
    ds = [jnp.where(allowed, p[h] * (dp[h] - sums[h]) * DH**-0.5, 0.0).astype(bf) for h in heads]
    wk = [jnp.where(i > j, mm(wb[h], k[h], 1, 1), 0.0) for h in heads]
    gram = [mm(wb[h], wb[h], 1, 1) for h in heads]
    dm = [(-mm(ds[h], (beta[h] * wk[h]).astype(bf), 1, 1)).astype(bf) for h in heads]
    dwk = [jnp.where(i > j, -mm(m[h], ds[h], 0, 0), 0.0) for h in heads]
    z = [mm(dm[h], x[h], 1, 1) for h in heads]
    dbeta = [jnp.sum(dwk[h] * wk[h], axis=1, keepdims=True) for h in heads]
    dwk = [(beta[h] * dwk[h]).astype(bf) for h in heads]
    da = [jnp.where(i > j, -mm(m[h], z[h].astype(bf), 0, 0), 0.0) for h in heads]
    dqw = [jnp.where(i >= j, z[h], 0.0).astype(bf) for h in heads]
    dbeta = [dbeta[h] + jnp.sum(da[h] * gram[h], axis=1, keepdims=True) for h in heads]
    dg = [(beta[h] * da[h]).astype(bf) for h in heads]
    dw = [mm(dg[h], wb[h], 1, 0) + mm(dg[h], wb[h], 0, 0) + mm(dqw[h], q[h], 0, 0) + mm(dwk[h], k[h], 1, 0) for h in heads]
    for h in heads:
        dq_ref[:, cols[h]] = (mm(ds[h], k[h], 1, 0) + mm(dqw[h], wb[h], 1, 0)).astype(bf)
        dk_ref[:, cols[h]] = (mm(ds[h], q[h], 0, 0) + mm(dwk[h], wb[h], 0, 0)).astype(bf)
    lane = lax.broadcasted_iota(jnp.int32, logits.shape, 1)
    out = jnp.zeros_like(logits)
    for h in heads:
        out = out + jnp.where(lane == base + h, dbeta[h] * (beta[h] * (1.0 - 0.5 * beta[h])), 0.0)
        r = dirs[h][1]
        dc = r * (dw[h] - w[h] * jnp.sum(w[h] * dw[h], axis=1, keepdims=True))
        taps = taps_ref[:, cols[h]]
        dpath = dc * taps[0:1]
        dtaps = [jnp.sum(dc * path[h], axis=0, keepdims=True)]
        for s in range(1, taps.shape[0]):
            up = shift_up(jnp.where(kept(dc.shape, s, first), dc, 0.0), s)
            dpath = dpath + up * taps[s : s + 1]
            dtaps.append(jnp.sum(up * path[h], axis=0, keepdims=True))
        dpath_ref[:, cols[h]] = dpath.astype(bf)
        dtaps_ref[:, cols[h]] = jnp.concatenate(dtaps, axis=0)

    @pl.when(pl.program_id(0) == 0)
    def _():
        dlogit_ref[...] = out

    @pl.when(pl.program_id(0) > 0)
    def _():
        dlogit_ref[...] += out


VM = 60 * 1024 * 1024


def specs(rows, ntaps, nh):
    wide = pl.BlockSpec((rows, HB * DH), lambda n: (0, n))
    square = pl.BlockSpec((HB, rows, rows), lambda n: (n, 0, 0))
    logit = pl.BlockSpec((rows, nh), lambda n: (0, 0))
    taps = pl.BlockSpec((ntaps, HB * DH), lambda n: (0, n))
    smem = pl.BlockSpec(memory_space=pltpu.SMEM)
    return wide, square, logit, taps, smem


def mix_forward(first, q, k, v, path, logit, taps):
    rows, width = q.shape
    nh = width // DH
    wide, square, lg, tp, sm = specs(rows, taps.shape[0], nh)
    sq = jax.ShapeDtypeStruct((nh, rows, rows), bf)
    return pl.pallas_call(
        forward_kernel,
        grid=(nh // HB,),
        in_specs=[sm, wide, wide, wide, wide, lg, tp],
        out_specs=[wide, square, square, square],
        out_shape=[jax.ShapeDtypeStruct((rows, width), bf), sq, sq, sq],
        compiler_params=pltpu.CompilerParams(vmem_limit_bytes=VM),
        cost_estimate=pl.CostEstimate(flops=10 * 10**9, bytes_accessed=6 * 10**6, transcendentals=0),
        name="mix_forward",
    )(first, q, k, v, path, logit, taps)


def mix_backward(first, q, k, v, path, logit, taps, x, m, p, do):
    rows, width = q.shape
    nh = width // DH
    wide, square, lg, tp, sm = specs(rows, taps.shape[0], nh)
    low = jax.ShapeDtypeStruct((rows, width), bf)
    return pl.pallas_call(
        backward_kernel,
        grid=(nh // HB,),
        in_specs=[sm, wide, wide, wide, wide, lg, tp, square, square, square, wide],
        out_specs=[wide, wide, wide, wide, lg, tp],
        out_shape=[low, low, low, low, jax.ShapeDtypeStruct((rows, nh), f32), jax.ShapeDtypeStruct(taps.shape, f32)],
        compiler_params=pltpu.CompilerParams(vmem_limit_bytes=VM),
        cost_estimate=pl.CostEstimate(flops=10 * 10**9, bytes_accessed=6 * 10**6, transcendentals=0),
        name="mix_backward",
    )(first, q, k, v, path, logit, taps, x, m, p, do)


def dot_trans(left, right):
    return lax.dot_general(left, right, (((1,), (1,)), ((), ())), preferred_element_type=f32)


def dot(left, right):
    return jnp.dot(left, right, preferred_element_type=f32)


def product_kernel(a0, a1, a2, a3, b0, b1, b2, b3, o_ref):
    total = mm(a0[...], b0[...], 1, 0) + mm(a1[...], b1[...], 1, 0)
    total = total + mm(a2[...], b2[...], 1, 0) + mm(a3[...], b3[...], 1, 0)
    o_ref[...] = total.astype(bf)


def product(lefts, rights):
    rows, slots = lefts[0].shape
    width = rights[0].shape[1]
    tile = 512 if width % 512 == 0 else 384
    return pl.pallas_call(
        product_kernel,
        grid=(width // tile,),
        in_specs=[pl.BlockSpec((rows, slots), lambda n: (0, 0))] * 4
        + [pl.BlockSpec((slots, tile), lambda n: (0, n))] * 4,
        out_specs=pl.BlockSpec((rows, tile), lambda n: (0, n)),
        out_shape=jax.ShapeDtypeStruct((rows, width), bf),
        compiler_params=pltpu.CompilerParams(vmem_limit_bytes=VM // 2),
        cost_estimate=pl.CostEstimate(
            flops=8 * rows * slots * width, bytes_accessed=2 * (4 * slots + rows) * (width + 4), transcendentals=0
        ),
        name="product",
    )(*lefts, *rights)


def pick(array, which, axis=0):
    return lax.dynamic_index_in_dim(array, which, axis, keepdims=False)


class Links:
    def __init__(self):
        self.count = lax.axis_size("dp")
        self.line = self.count // 4
        self.me = lax.axis_index("dp")
        self.core = self.me % 2
        self.pair = (self.me // 2) % 2
        self.place = self.me // 4

    def flip(self, array, bit):
        return lax.ppermute(array, "dp", [(i, i ^ bit) for i in range(self.count)])

    def left(self, array):
        slots = array.shape[0]
        rows = array.shape[1] // self.count
        turned = array.T.reshape(self.line, 2, 2, rows, slots)
        mine = pick(turned, self.pair, 1)
        theirs = self.flip(pick(turned, 1 - self.pair, 1), 2)
        away = jnp.stack([pick(mine, 1 - self.core, 1), pick(theirs, 1 - self.core, 1)])
        away = self.flip(away, 1)
        blocks = (pick(mine, self.core, 1), pick(theirs, self.core, 1), away[0], away[1])
        return [block.reshape(self.line * rows, slots) for block in blocks]

    def right(self, array):
        theirs = self.flip(array, 2)
        return [array, theirs, self.flip(array, 1), self.flip(theirs, 1)]

    def scatter(self, partial):
        n, z = self.line, self.place
        shards = partial.reshape(n, -1, partial.shape[1])
        up = down = None
        for s in range(1, n):
            send_up = pick(shards, jnp.clip(n + z - s, 0, n - 1))
            send_down = pick(shards, jnp.clip(s - n + z, 0, n - 1))
            if up is not None:
                send_up = send_up + up
                send_down = send_down + down
            rise = [(p * 4 + j, p * 4 + 4 + j) for p in range(s) for j in range(4)]
            fall = [((n - 1 - p) * 4 + j, (n - 2 - p) * 4 + j) for p in range(s) for j in range(4)]
            up = lax.ppermute(send_up, "dp", rise)
            down = lax.ppermute(send_down, "dp", fall)
        return pick(shards, z).astype(f32) + up.astype(f32) + down.astype(f32)

    def total(self, array):
        bit = 1
        while bit < self.count:
            array = array + self.flip(array, bit)
            bit *= 2
        return array


def swap(array):
    return lax.ppermute(array, "head", [(0, 1), (1, 0)])


def in_order(own, other, place):
    both = jnp.zeros((2,) + own.shape, own.dtype)
    both = lax.dynamic_update_index_in_dim(both, own, place, 0)
    return lax.dynamic_update_index_in_dim(both, other, 1 - place, 0)


def norm_back(grad, values, gain, scale):
    scaled = gain * grad
    mean = jnp.mean(scaled * values, axis=1, keepdims=True)
    return scale * scaled - values * (scale * scale * scale) * mean


def norm_scale(values):
    return lax.rsqrt(jnp.mean(values * values, axis=1, keepdims=True) + 1e-6)


def per_device(
    tokens,
    norm1_gain,
    w_query,
    w_key,
    w_value,
    w_path,
    w_beta,
    conv_kernel,
    w_output,
    norm2_gain,
    w_gate,
    w_up,
    w_down,
    item_lengths,
    cotangent,
):
    links = Links()
    head = lax.axis_index("head")
    local = tokens.shape[0]
    depth = tokens.shape[1]

    tokens_all = in_order(tokens, swap(tokens), head).reshape(2 * local, depth)
    cot_all = in_order(cotangent, swap(cotangent), head).reshape(2 * local, depth)

    quarter = 2 * links.pair + links.core
    quarters = w_output.reshape(4, depth // 4, w_output.shape[1])
    got = swap(pick(quarters, quarter))
    got = in_order(got, links.flip(got, 2), links.pair)
    got = in_order(got, links.flip(got, 1), links.core)
    w_output_other = jnp.swapaxes(got, 0, 1).reshape(w_output.shape)

    inputs = tokens_all.astype(f32)
    scale1 = norm_scale(inputs)
    normed1 = (inputs * scale1 * norm1_gain).astype(bf)
    queries = dot(normed1, w_query).astype(bf)
    keys = dot(normed1, w_key).astype(bf)
    values = dot(normed1, w_value).astype(bf)
    path_raw = dot(normed1, w_path)
    beta_logit = dot(normed1, w_beta)
    taps = jnp.transpose(conv_kernel, (2, 1, 0)).reshape(conv_kernel.shape[2], -1)
    mixed, solved, moved, probs = mix_forward(item_lengths, queries, keys, values, path_raw, beta_logit, taps)

    resid = inputs + dot_trans(mixed, w_output) + dot_trans(swap(mixed), w_output_other)
    scale2 = norm_scale(resid)
    normed2 = (resid * scale2 * norm2_gain).astype(bf)
    gate = dot(normed2, w_gate)
    upper = dot(normed2, w_up)
    sigma = jax.nn.sigmoid(gate)
    activated = gate * sigma
    hidden = (activated * upper).astype(bf)
    grad_hidden = dot(cot_all, w_down)
    grad_gate = (grad_hidden * upper * (sigma * (1.0 + gate * (1.0 - sigma)))).astype(bf)
    grad_upper = (grad_hidden * activated).astype(bf)
    part2 = dot_trans(grad_gate, w_gate) + dot_trans(grad_upper, w_up)
    grad_normed2 = part2 + swap(part2.astype(bf)).astype(f32)
    grad_gain2 = jnp.sum(grad_normed2 * resid * scale2, axis=0, keepdims=True)
    grad_resid = cot_all.astype(f32) + norm_back(grad_normed2, resid, norm2_gain, scale2)
    branch = grad_resid.astype(bf)
    grad_mixed = dot(branch, w_output).astype(bf)
    grad_q, grad_k, grad_v, grad_p, grad_logit, grad_taps = mix_backward(
        item_lengths, queries, keys, values, path_raw, beta_logit, taps, solved, moved, probs, grad_mixed
    )

    def halves(array):
        return array.reshape(2, local, depth)

    part = halves(dot_trans(hidden, w_down))
    ffn = pick(part, head) + swap(pick(part, 1 - head).astype(bf)).astype(f32)
    resid_own = pick(halves(resid), head)
    activations = (resid_own + ffn).astype(bf)

    low_logit = grad_logit.astype(bf)
    part = dot_trans(grad_q, w_query) + dot_trans(grad_k, w_key) + dot_trans(grad_v, w_value)
    part = halves(part + dot_trans(grad_p, w_path) + dot_trans(low_logit, w_beta))
    grad_normed1 = pick(part, head) + swap(pick(part, 1 - head).astype(bf)).astype(f32)
    inputs_own = tokens.astype(f32)
    scale_own = norm_scale(inputs_own)
    grad_tokens = pick(halves(grad_resid), head) + norm_back(grad_normed1, inputs_own, norm1_gain, scale_own)
    grad_gain1 = jnp.sum(grad_normed1 * inputs_own * scale_own, axis=0, keepdims=True)

    left_cot = links.left(cot_all)
    left_one = links.left(normed1)
    left_two = links.left(normed2)
    grad_w_down = links.scatter(product(left_cot, links.right(hidden)))
    grad_w_gate = links.scatter(product(left_two, links.right(grad_gate)))
    grad_w_up = links.scatter(product(left_two, links.right(grad_upper)))
    left_branch = links.left(branch)
    grad_w_output = links.scatter(product(left_branch, links.right(mixed)))
    width = w_query.shape[1]
    joined = links.scatter(product(left_one, links.right(jnp.concatenate([grad_q, grad_k], axis=1))))
    grad_w_query, grad_w_key = joined[:, :width], joined[:, width:]
    joined = links.scatter(product(left_one, links.right(jnp.concatenate([grad_v, grad_p], axis=1))))
    grad_w_value, grad_w_path = joined[:, :width], joined[:, width:]

    small = lax.dot_general(low_logit, normed1, (((0,), (0,)), ((), ())), preferred_element_type=f32)
    tall = jnp.zeros((grad_taps.shape[0], depth - width), f32)
    small = jnp.concatenate([small, grad_gain2, jnp.concatenate([grad_taps, tall], axis=1)], axis=0)
    small = links.total(small)
    heads = w_beta.shape[1]
    rows = depth // links.count
    grad_w_beta = lax.dynamic_slice_in_dim(small[:heads], rows * links.me, rows, 1).T
    piece = rows // 2
    grad_gain2 = lax.dynamic_slice_in_dim(small[heads], rows * links.me + piece * head, piece, 0)
    conv_rows = conv_kernel.shape[0] // links.count
    conv = small[heads + 1 :, :width].reshape(-1, heads, conv_kernel.shape[0])
    grad_conv = jnp.transpose(lax.dynamic_slice_in_dim(conv, conv_rows * links.me, conv_rows, 2), (2, 1, 0))
    grad_gain1 = links.total(grad_gain1 + swap(grad_gain1))
    grad_gain1 = lax.dynamic_slice_in_dim(grad_gain1[0], rows * links.me + piece * head, piece, 0)

    return (
        activations,
        grad_tokens,
        grad_gain1,
        grad_w_query,
        grad_w_key,
        grad_w_value,
        grad_w_path,
        grad_w_beta,
        grad_conv,
        grad_w_output,
        grad_gain2,
        grad_w_gate,
        grad_w_up,
        grad_w_down,
    )


def solution(mesh):
    in_specs = (
        P(("dp", "head"), None),
        P(),
        P(None, "head"),
        P(None, "head"),
        P(None, "head"),
        P(None, "head"),
        P(None, "head"),
        P(None, "head", None),
        P(None, "head"),
        P(),
        P(None, "head"),
        P(None, "head"),
        P(None, "head"),
        P("dp"),
        P(("dp", "head"), None),
    )
    out_specs = (
        P(("dp", "head"), None),
        P(("dp", "head"), None),
        P(("dp", "head")),
        P("dp", "head"),
        P("dp", "head"),
        P("dp", "head"),
        P("dp", "head"),
        P("dp", "head"),
        P("dp", "head", None),
        P("dp", "head"),
        P(("dp", "head")),
        P("dp", "head"),
        P("dp", "head"),
        P("dp", "head"),
    )
    return jax.shard_map(
        per_device, mesh=mesh, in_specs=in_specs, out_specs=out_specs, check_vma=False
    )
```

```python
import jax
import jax.numpy as jnp
from jax import lax
from jax.experimental import pallas as pl
from jax.experimental.pallas import tpu as pltpu
from jax.sharding import PartitionSpec as P

f32 = jnp.float32
bf = jnp.bfloat16
DH = 128
HB = 3


def mm(a, b, ca, cb):
    return lax.dot_general(a, b, (((ca,), (cb,)), ((), ())), preferred_element_type=f32)


def parts(a):
    high = a.astype(bf)
    return high, (a - high.astype(f32)).astype(bf)


def mm3(a, b, ca, cb):
    (ah, al), (bh, bl) = a, b
    return mm(ah, bh, ca, cb) + mm(ah, bl, ca, cb) + mm(al, bh, ca, cb)


def mm2(a, b, ca, cb):
    return mm(a, b[0], ca, cb) + mm(a, b[1], ca, cb)


def index(shape):
    return lax.broadcasted_iota(jnp.int32, shape, 0), lax.broadcasted_iota(jnp.int32, shape, 1)


def column(array, which):
    lane = lax.broadcasted_iota(jnp.int32, array.shape, 1)
    return jnp.sum(jnp.where(lane == which, array, 0.0), axis=1, keepdims=True)


def shift_down(a, s):
    return jnp.concatenate([jnp.zeros((s, a.shape[1]), a.dtype), a[: a.shape[0] - s]], axis=0)


def shift_up(a, s):
    return jnp.concatenate([a[s:], jnp.zeros((s, a.shape[1]), a.dtype)], axis=0)


def kept(shape, s, first):
    t = lax.broadcasted_iota(jnp.int32, shape, 0)
    return (t >= s) & ~((t >= first) & (t - s < first))


def directions(path, taps, first):
    total = path * taps[0:1]
    for s in range(1, taps.shape[0]):
        total = total + jnp.where(kept(path.shape, s, first), shift_down(path, s), 0.0) * taps[s : s + 1]
    r = lax.rsqrt(jnp.sum(total * total, axis=1, keepdims=True) + 1e-6)
    return total * r, r


def inverses(systems):
    size = systems[0].shape[0]
    i, j = index((size, size))
    solved = [jnp.where(i == j, 1.0, 0.0) - jnp.where(i // 2 == j // 2, a, 0.0) for a in systems]
    width = 2
    while width < size:
        inside = (i // (2 * width) == j // (2 * width)) & (i // width != j // width)
        offs = [parts(jnp.where(inside, a, 0.0)) for a in systems]
        lows = [parts(x) for x in solved]
        inner = [parts(mm3(o, x, 1, 0)) for o, x in zip(offs, lows)]
        solved = [x - mm3(l, y, 1, 0) for x, l, y in zip(solved, lows, inner)]
        width *= 2
    return solved


def forward_kernel(first_ref, q_ref, k_ref, v_ref, path_ref, logit_ref, taps_ref, o_ref, x_ref, m_ref, p_ref):
    first = first_ref[0]
    rows = q_ref.shape[0]
    half = rows // 2
    base = pl.program_id(0) * HB
    heads = range(HB)
    cols = [slice(h * DH, (h + 1) * DH) for h in heads]
    i, j = index((rows, rows))
    q = [q_ref[:, c] for c in cols]
    k = [k_ref[:, c] for c in cols]
    w = [parts(directions(path_ref[:, c], taps_ref[:, c], first)[0]) for c in cols]
    logits = logit_ref[...]
    beta = [2.0 * jax.nn.sigmoid(column(logits, base + h)) for h in heads]
    system = [jnp.where(i > j, beta[h] * mm3(w[h], w[h], 1, 1), 0.0) for h in heads]
    corners = inverses([s[:half, :half] for s in system] + [s[half:, half:] for s in system])
    corners = [parts(x) for x in corners]
    low = [parts(mm3(parts(system[h][half:, :half]), corners[h], 1, 0)) for h in heads]
    low = [parts(-mm3(corners[HB + h], low[h], 1, 0)) for h in heads]
    zero = jnp.zeros((half, half), bf)
    x = [
        tuple(
            jnp.concatenate(
                [
                    jnp.concatenate([corners[h][n], zero], axis=1),
                    jnp.concatenate([low[h][n], corners[HB + h][n]], axis=1),
                ],
                axis=0,
            )
            for n in range(2)
        )
        for h in heads
    ]
    qw = [parts(jnp.where(i >= j, mm2(q[h], w[h], 1, 1), 0.0)) for h in heads]
    wk = [mm(w[h][0], k[h], 1, 1) + mm(w[h][1], k[h], 1, 1) for h in heads]
    wk = [parts(jnp.where(i > j, beta[h] * wk[h], 0.0)) for h in heads]
    m = [parts(mm3(qw[h], x[h], 1, 0)) for h in heads]
    s = [mm(q[h], k[h], 1, 1) - mm3(m[h], wk[h], 1, 0) for h in heads]
    allowed = (i >= j) & ((i < first) | (j >= first))
    s = [jnp.where(allowed, a * DH**-0.5, -1e30) for a in s]
    e = [jnp.exp(a - jnp.max(a, axis=1, keepdims=True)) for a in s]
    p = [(a / jnp.sum(a, axis=1, keepdims=True)).astype(bf) for a in e]
    for h in heads:
        o_ref[:, cols[h]] = mm(p[h], v_ref[:, cols[h]], 1, 0).astype(bf)
        x_ref[h] = x[h][0]
        m_ref[h] = m[h][0]
        p_ref[h] = p[h]


def backward_kernel(
    first_ref, q_ref, k_ref, v_ref, path_ref, logit_ref, taps_ref, x_ref, m_ref, p_ref, do_ref,
    dq_ref, dk_ref, dv_ref, dpath_ref, dlogit_ref, dtaps_ref,
):
    first = first_ref[0]
    rows = q_ref.shape[0]
    base = pl.program_id(0) * HB
    heads = range(HB)
    cols = [slice(h * DH, (h + 1) * DH) for h in heads]
    i, j = index((rows, rows))
    allowed = (i >= j) & ((i < first) | (j >= first))
    q = [q_ref[:, c] for c in cols]
    k = [k_ref[:, c] for c in cols]
    do = [do_ref[:, c].astype(bf) for c in cols]
    path = [path_ref[:, c] for c in cols]
    dirs = [directions(path[h], taps_ref[:, cols[h]], first) for h in heads]
    w = [d[0] for d in dirs]
    wb = [a.astype(bf) for a in w]
    logits = logit_ref[...]
    beta = [2.0 * jax.nn.sigmoid(column(logits, base + h)) for h in heads]
    p = [p_ref[h] for h in heads]
    x = [x_ref[h] for h in heads]
    m = [m_ref[h] for h in heads]
    dp = [mm(do[h], v_ref[:, cols[h]], 1, 1) for h in heads]
    for h in heads:
        dv_ref[:, cols[h]] = mm(p[h], do[h], 0, 0).astype(bf)
    p = [a.astype(f32) for a in p]
    sums = [jnp.sum(dp[h] * p[h], axis=1, keepdims=True) for h in heads]
    ds = [jnp.where(allowed, p[h] * (dp[h] - sums[h]) * DH**-0.5, 0.0).astype(bf) for h in heads]
    wk = [jnp.where(i > j, mm(wb[h], k[h], 1, 1), 0.0) for h in heads]
    gram = [mm(wb[h], wb[h], 1, 1) for h in heads]
    dm = [(-mm(ds[h], (beta[h] * wk[h]).astype(bf), 1, 1)).astype(bf) for h in heads]
    dwk = [jnp.where(i > j, -mm(m[h], ds[h], 0, 0), 0.0) for h in heads]
    z = [mm(dm[h], x[h], 1, 1) for h in heads]
    dbeta = [jnp.sum(dwk[h] * wk[h], axis=1, keepdims=True) for h in heads]
    dwk = [(beta[h] * dwk[h]).astype(bf) for h in heads]
    da = [jnp.where(i > j, -mm(m[h], z[h].astype(bf), 0, 0), 0.0) for h in heads]
    dqw = [jnp.where(i >= j, z[h], 0.0).astype(bf) for h in heads]
    dbeta = [dbeta[h] + jnp.sum(da[h] * gram[h], axis=1, keepdims=True) for h in heads]
    dg = [(beta[h] * da[h]).astype(bf) for h in heads]
    dw = [mm(dg[h], wb[h], 1, 0) + mm(dg[h], wb[h], 0, 0) + mm(dqw[h], q[h], 0, 0) + mm(dwk[h], k[h], 1, 0) for h in heads]
    for h in heads:
        dq_ref[:, cols[h]] = (mm(ds[h], k[h], 1, 0) + mm(dqw[h], wb[h], 1, 0)).astype(bf)
        dk_ref[:, cols[h]] = (mm(ds[h], q[h], 0, 0) + mm(dwk[h], wb[h], 0, 0)).astype(bf)
    lane = lax.broadcasted_iota(jnp.int32, logits.shape, 1)
    out = jnp.zeros_like(logits)
    for h in heads:
        out = out + jnp.where(lane == base + h, dbeta[h] * (beta[h] * (1.0 - 0.5 * beta[h])), 0.0)
        r = dirs[h][1]
        dc = r * (dw[h] - w[h] * jnp.sum(w[h] * dw[h], axis=1, keepdims=True))
        taps = taps_ref[:, cols[h]]
        dpath = dc * taps[0:1]
        dtaps = [jnp.sum(dc * path[h], axis=0, keepdims=True)]
        for s in range(1, taps.shape[0]):
            up = shift_up(jnp.where(kept(dc.shape, s, first), dc, 0.0), s)
            dpath = dpath + up * taps[s : s + 1]
            dtaps.append(jnp.sum(up * path[h], axis=0, keepdims=True))
        dpath_ref[:, cols[h]] = dpath.astype(bf)
        dtaps_ref[:, cols[h]] = jnp.concatenate(dtaps, axis=0)

    @pl.when(pl.program_id(0) == 0)
    def _():
        dlogit_ref[...] = out

    @pl.when(pl.program_id(0) > 0)
    def _():
        dlogit_ref[...] += out


VM = 60 * 1024 * 1024


def specs(rows, ntaps, nh):
    wide = pl.BlockSpec((rows, HB * DH), lambda n: (0, n))
    square = pl.BlockSpec((HB, rows, rows), lambda n: (n, 0, 0))
    logit = pl.BlockSpec((rows, nh), lambda n: (0, 0))
    taps = pl.BlockSpec((ntaps, HB * DH), lambda n: (0, n))
    smem = pl.BlockSpec(memory_space=pltpu.SMEM)
    return wide, square, logit, taps, smem


def mix_forward(first, q, k, v, path, logit, taps):
    rows, width = q.shape
    nh = width // DH
    wide, square, lg, tp, sm = specs(rows, taps.shape[0], nh)
    sq = jax.ShapeDtypeStruct((nh, rows, rows), bf)
    return pl.pallas_call(
        forward_kernel,
        grid=(nh // HB,),
        in_specs=[sm, wide, wide, wide, wide, lg, tp],
        out_specs=[wide, square, square, square],
        out_shape=[jax.ShapeDtypeStruct((rows, width), bf), sq, sq, sq],
        compiler_params=pltpu.CompilerParams(vmem_limit_bytes=VM),
        cost_estimate=pl.CostEstimate(flops=1, bytes_accessed=1, transcendentals=0),
        name="mix_forward",
    )(first, q, k, v, path, logit, taps)


def mix_backward(first, q, k, v, path, logit, taps, x, m, p, do):
    rows, width = q.shape
    nh = width // DH
    wide, square, lg, tp, sm = specs(rows, taps.shape[0], nh)
    low = jax.ShapeDtypeStruct((rows, width), bf)
    return pl.pallas_call(
        backward_kernel,
        grid=(nh // HB,),
        in_specs=[sm, wide, wide, wide, wide, lg, tp, square, square, square, wide],
        out_specs=[wide, wide, wide, wide, lg, tp],
        out_shape=[low, low, low, low, jax.ShapeDtypeStruct((rows, nh), f32), jax.ShapeDtypeStruct(taps.shape, f32)],
        compiler_params=pltpu.CompilerParams(vmem_limit_bytes=VM),
        cost_estimate=pl.CostEstimate(flops=1, bytes_accessed=1, transcendentals=0),
        name="mix_backward",
    )(first, q, k, v, path, logit, taps, x, m, p, do)


def dot_trans(left, right):
    return lax.dot_general(left, right, (((1,), (1,)), ((), ())), preferred_element_type=f32)


def dot(left, right):
    return jnp.dot(left, right, preferred_element_type=f32)


def product_kernel(near, far, b0, b1, b2, b3, away_ref, keep_ref):
    total = mm(near[0], b0[...], 1, 0) + mm(near[1], b1[...], 1, 0)
    total = (total + mm(far[0], b2[...], 1, 0) + mm(far[1], b3[...], 1, 0)).astype(bf)
    half = total.shape[0] // 2
    away_ref[...] = total[:half]
    keep_ref[...] = total[half:]


def product(left, rights):
    near, far = left
    sources, rows, slots = near.shape
    width = rights[0].shape[1]
    tile = 512 if width % 512 == 0 else 384
    half = jax.ShapeDtypeStruct((rows // 2, width), bf)
    return pl.pallas_call(
        product_kernel,
        grid=(width // tile,),
        in_specs=[pl.BlockSpec((sources, rows, slots), lambda n: (0, 0, 0))] * 2
        + [pl.BlockSpec((slots, tile), lambda n: (0, n))] * 4,
        out_specs=[pl.BlockSpec((rows // 2, tile), lambda n: (0, n))] * 2,
        out_shape=[half, half],
        compiler_params=pltpu.CompilerParams(vmem_limit_bytes=VM // 2),
        cost_estimate=pl.CostEstimate(flops=1, bytes_accessed=1, transcendentals=0),
        name="product",
    )(near, far, *rights)


def turn_kernel(blocks_ref, own_ref, core_ref, near_ref, far_ref, turned):
    count = near_ref.shape[1] // blocks_ref.shape[1]
    for source, ref in enumerate((own_ref, core_ref)):
        for n in range(ref.shape[1] // DH):
            turned[n * DH : (n + 1) * DH, :] = ref[:, n * DH : (n + 1) * DH].T
        for which, out in enumerate((near_ref, far_ref)):
            for n in range(blocks_ref.shape[1]):
                start = pl.multiple_of(blocks_ref[which, n] * count, 16)
                out[source, n * count : (n + 1) * count, :] = turned[pl.ds(start, count), :]


def turn(blocks, own, core):
    slots, features = own.shape
    rows = features // 4
    out = jax.ShapeDtypeStruct((2, rows, slots), bf)
    per = rows // blocks.shape[1]
    if per % 16:
        both = jnp.stack([own.T, core.T]).reshape(2, features // per, per, slots)
        return [both[:, blocks[n]].reshape(2, rows, slots) for n in range(2)]
    vmem = pl.BlockSpec(memory_space=pltpu.VMEM)
    return pl.pallas_call(
        turn_kernel,
        in_specs=[pl.BlockSpec(memory_space=pltpu.SMEM), vmem, vmem],
        out_specs=[vmem, vmem],
        out_shape=[out, out],
        scratch_shapes=[pltpu.VMEM((features, slots), bf)],
        compiler_params=pltpu.CompilerParams(vmem_limit_bytes=VM // 2),
        cost_estimate=pl.CostEstimate(flops=1, bytes_accessed=1, transcendentals=0),
        name="turn",
    )(blocks, own, core)


def after(array, *others):
    return lax.optimization_barrier((array,) + others)[0]


def pick(array, which, axis=0):
    return lax.dynamic_index_in_dim(array, which, axis, keepdims=False)


class Links:
    def __init__(self):
        self.count = lax.axis_size("dp")
        self.line = self.count // 4
        self.me = lax.axis_index("dp")
        self.core = self.me % 2
        self.pair = (self.me // 2) % 2
        self.place = self.me // 4
        places = [self.place]
        bit = self.line // 2
        while bit >= 1:
            places = [p ^ bit for p in places] + places
            bit //= 2
        chips = jnp.stack(places) * 4 + self.core
        self.blocks = jnp.stack([chips + 2 * self.pair, chips + 2 * (1 - self.pair)]).astype(jnp.int32)

    def flip(self, array, bit):
        return lax.ppermute(array, "dp", [(i, i ^ bit) for i in range(self.count)])

    def left(self, array, *before):
        near, away = turn(self.blocks, array, self.flip(array, 1))
        return near, self.flip(after(away, *before), 2)

    def pair_rows(self, array, *before):
        return self.flip(after(array, *before), 2)

    def right(self, array, theirs):
        return [array, self.flip(array, 1), theirs, self.flip(theirs, 1)]

    def scatter(self, halves):
        away, keep = halves
        bit, first = 1, None
        while True:
            got = self.flip(away, 4 * bit)
            bit *= 2
            if bit == self.line:
                return keep.astype(f32) + got.astype(f32), first
            half = keep.shape[0] // 2
            away = keep[:half] + got[:half]
            keep = keep[half:] + got[half:]
            if first is None:
                first = away


def swap(array):
    return lax.ppermute(array, "head", [(0, 1), (1, 0)])


def in_order(own, other, place):
    return jnp.concatenate([jnp.where(place == 0, own, other), jnp.where(place == 0, other, own)], axis=0)


def norm_back(grad, values, gain, scale):
    scaled = gain * grad
    mean = jnp.mean(scaled * values, axis=1, keepdims=True)
    return scale * scaled - values * (scale * scale * scale) * mean


def norm_scale(values):
    return lax.rsqrt(jnp.mean(values * values, axis=1, keepdims=True) + 1e-6)


def per_device(
    tokens,
    norm1_gain,
    w_query,
    w_key,
    w_value,
    w_path,
    w_beta,
    conv_kernel,
    w_output,
    norm2_gain,
    w_gate,
    w_up,
    w_down,
    item_lengths,
    cotangent,
):
    links = Links()
    head = lax.axis_index("head")
    local = tokens.shape[0]
    depth = tokens.shape[1]

    tokens_other = swap(tokens)
    tokens_all = in_order(tokens, tokens_other, head)

    quarter = 2 * links.pair + links.core
    quarters = w_output.reshape(4, depth // 4, w_output.shape[1])
    cot_other = swap(after(cotangent, tokens_other))
    cot_all = in_order(cotangent, cot_other, head)
    got = swap(after(pick(quarters, quarter), cot_other))

    inputs = tokens_all.astype(f32)
    scale1 = norm_scale(inputs)
    normed1 = (inputs * scale1 * norm1_gain).astype(bf)
    queries = dot(normed1, w_query).astype(bf)
    keys = dot(normed1, w_key).astype(bf)
    values = dot(normed1, w_value).astype(bf)
    path_raw = dot(normed1, w_path)
    beta_logit = dot(normed1, w_beta)
    taps = jnp.transpose(conv_kernel, (2, 1, 0)).reshape(conv_kernel.shape[2], -1)

    queries = after(queries, cot_other)
    left_cot = links.left(cot_all)
    mixed, solved, moved, probs = mix_forward(item_lengths, queries, keys, values, path_raw, beta_logit, taps)
    got_pair = links.flip(after(got, mixed), 2)
    mixed_other = swap(mixed)
    got_core = links.flip(jnp.stack([got, got_pair]), 1)

    def chosen(pair, core):
        near = jnp.where(core == links.core, got, got_core[0])
        far = jnp.where(core == links.core, got_pair, got_core[1])
        return jnp.where(pair == links.pair, near, far)

    w_output_other = jnp.concatenate([chosen(0, 0), chosen(0, 1), chosen(1, 0), chosen(1, 1)], axis=0)
    resid = inputs + dot_trans(mixed, w_output) + dot_trans(mixed_other, w_output_other)
    scale2 = norm_scale(resid)
    normed2 = (resid * scale2 * norm2_gain).astype(bf)
    left_one = links.left(normed1, got_pair)
    left_two = links.left(normed2, left_one[1])
    gate = dot(normed2, w_gate)
    upper = dot(normed2, w_up)
    sigma = jax.nn.sigmoid(gate)
    activated = gate * sigma
    gate, upper, hidden = lax.optimization_barrier((gate, upper, (activated * upper).astype(bf)))
    sigma = jax.nn.sigmoid(gate)
    activated = gate * sigma
    grad_hidden = dot(cot_all, w_down)
    grad_gate = (grad_hidden * upper * (sigma * (1.0 + gate * (1.0 - sigma)))).astype(bf)
    grad_upper = (grad_hidden * activated).astype(bf)

    middle = hidden.shape[1] // 2
    hidden_parts = [hidden[:, :middle], hidden[:, middle:]]
    pairs_down0 = links.pair_rows(hidden_parts[0], left_one[1])
    part2 = dot_trans(grad_gate, w_gate) + dot_trans(grad_upper, w_up)
    other2 = swap(part2.astype(bf))
    pairs_down1 = links.pair_rows(hidden_parts[1], left_two[1])
    pairs_gate = links.pair_rows(grad_gate, pairs_down0)
    product_down0 = product(left_cot, links.right(hidden_parts[0], pairs_down0))
    sum_down0, first_down0 = links.scatter(product_down0)

    grad_normed2 = part2 + other2.astype(f32)
    grad_gain2 = jnp.sum(grad_normed2 * resid * scale2, axis=0, keepdims=True)
    grad_resid = cot_all.astype(f32) + norm_back(grad_normed2, resid, norm2_gain, scale2)
    branch = grad_resid.astype(bf)
    grad_mixed = dot(branch, w_output).astype(bf)
    product_down1 = product(left_cot, links.right(hidden_parts[1], pairs_down1))
    sum_down1, first_down1 = links.scatter(product_down1)

    grad_mixed = after(grad_mixed, product_down1[0])
    grad_q, grad_k, grad_v, grad_p, grad_logit, grad_taps = mix_backward(
        item_lengths, queries, keys, values, path_raw, beta_logit, taps, solved, moved, probs, grad_mixed
    )
    rights_qk = jnp.concatenate([grad_q, grad_k], axis=1)
    rights_vp = jnp.concatenate([grad_v, grad_p], axis=1)

    def halves(array):
        return array.reshape(2, local, depth)

    part = halves(dot_trans(hidden, w_down))
    ffn = swap(after(pick(part, 1 - head).astype(bf), other2))
    resid_own = pick(halves(resid), head)
    activations = (resid_own + pick(part, head) + ffn.astype(f32)).astype(bf)

    product_gate = product(left_two, links.right(grad_gate, pairs_gate))
    sum_gate, first_gate = links.scatter(product_gate)
    pairs_mixed = links.pair_rows(mixed, left_two[1])
    left_branch = links.left(branch, pairs_down1)
    pairs_up = links.pair_rows(grad_upper, left_branch[1], first_down0)
    product_output = product(left_branch, links.right(mixed, pairs_mixed))
    sum_output, first_output = links.scatter(product_output)
    product_up = product(left_two, links.right(grad_upper, pairs_up))
    sum_up, first_up = links.scatter(product_up)

    low_logit = grad_logit.astype(bf)
    part = dot_trans(grad_q, w_query) + dot_trans(grad_k, w_key) + dot_trans(grad_v, w_value)
    part = halves(part + dot_trans(grad_p, w_path) + dot_trans(low_logit, w_beta))
    other1 = swap(after(pick(part, 1 - head).astype(bf), ffn))
    grad_normed1 = pick(part, head) + other1.astype(f32)
    inputs_own = tokens.astype(f32)
    scale_own = norm_scale(inputs_own)
    grad_tokens = pick(halves(grad_resid), head) + norm_back(grad_normed1, inputs_own, norm1_gain, scale_own)
    grad_gain1 = jnp.sum(grad_normed1 * inputs_own * scale_own, axis=0, keepdims=True)

    pairs_qk = links.pair_rows(rights_qk, pairs_gate, first_gate)
    product_qk = product(left_one, links.right(rights_qk, pairs_qk))
    sum_qk, first_qk = links.scatter(product_qk)
    pairs_vp = links.pair_rows(rights_vp, pairs_up, first_output)
    product_vp = product(left_one, links.right(rights_vp, pairs_vp))
    sum_vp, first_vp = links.scatter(product_vp)

    width = w_query.shape[1]
    small = lax.dot_general(low_logit, normed1, (((0,), (0,)), ((), ())), preferred_element_type=f32)
    grad_gain1 = grad_gain1 + swap(grad_gain1)
    small = jnp.concatenate([small, grad_gain1, grad_gain2], axis=0)
    heads = w_beta.shape[1]
    rows = depth // links.count
    conv_rows = conv_kernel.shape[0] // links.count
    small = jnp.swapaxes(small.reshape(-1, links.count, rows), 0, 1)
    conv = jnp.swapaxes(grad_taps.reshape(-1, links.count, conv_rows), 0, 1).reshape(links.count, 2, rows)
    small = jnp.concatenate([small, conv], axis=1)
    small = jnp.pad(small, ((0, 0), (0, 16 - small.shape[1]), (0, DH - rows))).reshape(-1, DH)
    small = lax.psum_scatter(small, "dp", scatter_dimension=0, tiled=True)[:, :rows]
    small = after(small, first_vp)
    grad_w_beta = small[:heads].T
    piece = rows // 2
    gains = lax.dynamic_slice_in_dim(small[heads : heads + 2], piece * head, piece, 1)
    conv = small[heads + 2 : heads + 4].reshape(-1, heads, conv_rows)
    grad_conv = jnp.transpose(conv, (2, 1, 0))

    grad_gain1, grad_gain2 = gains[0], gains[1]
    grad_w_down = jnp.concatenate([sum_down0, sum_down1], axis=1)
    grad_w_gate, grad_w_up, grad_w_output = sum_gate, sum_up, sum_output
    grad_w_query, grad_w_key = sum_qk[:, :width], sum_qk[:, width:]
    grad_w_value, grad_w_path = sum_vp[:, :width], sum_vp[:, width:]
    return (
        activations,
        grad_tokens,
        grad_gain1,
        grad_w_query,
        grad_w_key,
        grad_w_value,
        grad_w_path,
        grad_w_beta,
        grad_conv,
        grad_w_output,
        grad_gain2,
        grad_w_gate,
        grad_w_up,
        grad_w_down,
    )


def solution(mesh):
    in_specs = (
        P(("dp", "head"), None),
        P(),
        P(None, "head"),
        P(None, "head"),
        P(None, "head"),
        P(None, "head"),
        P(None, "head"),
        P(None, "head", None),
        P(None, "head"),
        P(),
        P(None, "head"),
        P(None, "head"),
        P(None, "head"),
        P("dp"),
        P(("dp", "head"), None),
    )
    out_specs = (
        P(("dp", "head"), None),
        P(("dp", "head"), None),
        P(("dp", "head")),
        P("dp", "head"),
        P("dp", "head"),
        P("dp", "head"),
        P("dp", "head"),
        P("dp", "head"),
        P("dp", "head", None),
        P("dp", "head"),
        P(("dp", "head")),
        P("dp", "head"),
        P("dp", "head"),
        P("dp", "head"),
    )
    return jax.shard_map(
        per_device, mesh=mesh, in_specs=in_specs, out_specs=out_specs, check_vma=False
    )
```

```python
import jax
import jax.numpy as jnp
from jax import lax
from jax.experimental import pallas as pl
from jax.experimental.pallas import tpu as pltpu
from jax.sharding import PartitionSpec as P

f32 = jnp.float32
bf = jnp.bfloat16
DH = 128
HB = 3


def mm(a, b, ca, cb):
    return lax.dot_general(a, b, (((ca,), (cb,)), ((), ())), preferred_element_type=f32)


def parts(a):
    high = a.astype(bf)
    return high, (a - high.astype(f32)).astype(bf)


def mm3(a, b, ca, cb):
    (ah, al), (bh, bl) = a, b
    return mm(ah, bh, ca, cb) + mm(ah, bl, ca, cb) + mm(al, bh, ca, cb)


def mm2(a, b, ca, cb):
    return mm(a, b[0], ca, cb) + mm(a, b[1], ca, cb)


def index(shape):
    return lax.broadcasted_iota(jnp.int32, shape, 0), lax.broadcasted_iota(jnp.int32, shape, 1)


def column(array, which):
    lane = lax.broadcasted_iota(jnp.int32, array.shape, 1)
    return jnp.sum(jnp.where(lane == which, array, 0.0), axis=1, keepdims=True)


def shift_down(a, s):
    return jnp.concatenate([jnp.zeros((s, a.shape[1]), a.dtype), a[: a.shape[0] - s]], axis=0)


def shift_up(a, s):
    return jnp.concatenate([a[s:], jnp.zeros((s, a.shape[1]), a.dtype)], axis=0)


def kept(shape, s, first):
    t = lax.broadcasted_iota(jnp.int32, shape, 0)
    return (t >= s) & ~((t >= first) & (t - s < first))


def directions(path, taps, first):
    total = path * taps[0:1]
    for s in range(1, taps.shape[0]):
        total = total + jnp.where(kept(path.shape, s, first), shift_down(path, s), 0.0) * taps[s : s + 1]
    r = lax.rsqrt(jnp.sum(total * total, axis=1, keepdims=True) + 1e-6)
    return total * r, r


def inverses(systems):
    size = systems[0].shape[0]
    i, j = index((size, size))
    solved = [jnp.where(i == j, 1.0, 0.0) - jnp.where(i // 2 == j // 2, a, 0.0) for a in systems]
    width = 2
    while width < size:
        inside = (i // (2 * width) == j // (2 * width)) & (i // width != j // width)
        offs = [parts(jnp.where(inside, a, 0.0)) for a in systems]
        lows = [parts(x) for x in solved]
        inner = [parts(mm3(o, x, 1, 0)) for o, x in zip(offs, lows)]
        solved = [x - mm3(l, y, 1, 0) for x, l, y in zip(solved, lows, inner)]
        width *= 2
    return solved


def forward_kernel(first_ref, q_ref, k_ref, v_ref, path_ref, logit_ref, taps_ref, o_ref, x_ref, m_ref, p_ref):
    first = first_ref[0]
    rows = q_ref.shape[0]
    half = rows // 2
    base = pl.program_id(0) * HB
    heads = range(HB)
    cols = [slice(h * DH, (h + 1) * DH) for h in heads]
    i, j = index((rows, rows))
    q = [q_ref[:, c] for c in cols]
    k = [k_ref[:, c] for c in cols]
    w = [parts(directions(path_ref[:, c], taps_ref[:, c], first)[0]) for c in cols]
    logits = logit_ref[...]
    beta = [2.0 * jax.nn.sigmoid(column(logits, base + h)) for h in heads]
    system = [jnp.where(i > j, beta[h] * mm3(w[h], w[h], 1, 1), 0.0) for h in heads]
    corners = inverses([s[:half, :half] for s in system] + [s[half:, half:] for s in system])
    corners = [parts(x) for x in corners]
    low = [parts(mm3(parts(system[h][half:, :half]), corners[h], 1, 0)) for h in heads]
    low = [parts(-mm3(corners[HB + h], low[h], 1, 0)) for h in heads]
    zero = jnp.zeros((half, half), bf)
    x = [
        tuple(
            jnp.concatenate(
                [
                    jnp.concatenate([corners[h][n], zero], axis=1),
                    jnp.concatenate([low[h][n], corners[HB + h][n]], axis=1),
                ],
                axis=0,
            )
            for n in range(2)
        )
        for h in heads
    ]
    qw = [parts(jnp.where(i >= j, mm2(q[h], w[h], 1, 1), 0.0)) for h in heads]
    wk = [mm(w[h][0], k[h], 1, 1) + mm(w[h][1], k[h], 1, 1) for h in heads]
    wk = [parts(jnp.where(i > j, beta[h] * wk[h], 0.0)) for h in heads]
    m = [parts(mm3(qw[h], x[h], 1, 0)) for h in heads]
    s = [mm(q[h], k[h], 1, 1) - mm3(m[h], wk[h], 1, 0) for h in heads]
    allowed = (i >= j) & ((i < first) | (j >= first))
    s = [jnp.where(allowed, a * DH**-0.5, -1e30) for a in s]
    e = [jnp.exp(a - jnp.max(a, axis=1, keepdims=True)) for a in s]
    p = [(a / jnp.sum(a, axis=1, keepdims=True)).astype(bf) for a in e]
    for h in heads:
        o_ref[:, cols[h]] = mm(p[h], v_ref[:, cols[h]], 1, 0).astype(bf)
        x_ref[h] = x[h][0]
        m_ref[h] = m[h][0]
        p_ref[h] = p[h]


def backward_kernel(
    first_ref, q_ref, k_ref, v_ref, path_ref, logit_ref, taps_ref, x_ref, m_ref, p_ref, do_ref,
    dqk_ref, dvp_ref, dlogit_ref, dtaps_ref,
):
    first = first_ref[0]
    rows = q_ref.shape[0]
    base = pl.program_id(0) * HB
    heads = range(HB)
    cols = [slice(h * DH, (h + 1) * DH) for h in heads]
    i, j = index((rows, rows))
    allowed = (i >= j) & ((i < first) | (j >= first))
    q = [q_ref[:, c] for c in cols]
    k = [k_ref[:, c] for c in cols]
    do = [do_ref[:, c].astype(bf) for c in cols]
    path = [path_ref[:, c] for c in cols]
    dirs = [directions(path[h], taps_ref[:, cols[h]], first) for h in heads]
    w = [d[0] for d in dirs]
    wb = [a.astype(bf) for a in w]
    logits = logit_ref[...]
    beta = [2.0 * jax.nn.sigmoid(column(logits, base + h)) for h in heads]
    p = [p_ref[h] for h in heads]
    x = [x_ref[h] for h in heads]
    m = [m_ref[h] for h in heads]
    dp = [mm(do[h], v_ref[:, cols[h]], 1, 1) for h in heads]
    for h in heads:
        dvp_ref[0, :, cols[h]] = mm(p[h], do[h], 0, 0).astype(bf)
    p = [a.astype(f32) for a in p]
    sums = [jnp.sum(dp[h] * p[h], axis=1, keepdims=True) for h in heads]
    ds = [jnp.where(allowed, p[h] * (dp[h] - sums[h]) * DH**-0.5, 0.0).astype(bf) for h in heads]
    wk = [jnp.where(i > j, mm(wb[h], k[h], 1, 1), 0.0) for h in heads]
    gram = [mm(wb[h], wb[h], 1, 1) for h in heads]
    dm = [(-mm(ds[h], (beta[h] * wk[h]).astype(bf), 1, 1)).astype(bf) for h in heads]
    dwk = [jnp.where(i > j, -mm(m[h], ds[h], 0, 0), 0.0) for h in heads]
    z = [mm(dm[h], x[h], 1, 1) for h in heads]
    dbeta = [jnp.sum(dwk[h] * wk[h], axis=1, keepdims=True) for h in heads]
    dwk = [(beta[h] * dwk[h]).astype(bf) for h in heads]
    da = [jnp.where(i > j, -mm(m[h], z[h].astype(bf), 0, 0), 0.0) for h in heads]
    dqw = [jnp.where(i >= j, z[h], 0.0).astype(bf) for h in heads]
    dbeta = [dbeta[h] + jnp.sum(da[h] * gram[h], axis=1, keepdims=True) for h in heads]
    dg = [(beta[h] * da[h]).astype(bf) for h in heads]
    dw = [mm(dg[h], wb[h], 1, 0) + mm(dg[h], wb[h], 0, 0) + mm(dqw[h], q[h], 0, 0) + mm(dwk[h], k[h], 1, 0) for h in heads]
    for h in heads:
        dqk_ref[0, :, cols[h]] = (mm(ds[h], k[h], 1, 0) + mm(dqw[h], wb[h], 1, 0)).astype(bf)
        dqk_ref[1, :, cols[h]] = (mm(ds[h], q[h], 0, 0) + mm(dwk[h], wb[h], 0, 0)).astype(bf)
    lane = lax.broadcasted_iota(jnp.int32, logits.shape, 1)
    out = jnp.zeros_like(logits)
    for h in heads:
        out = out + jnp.where(lane == base + h, dbeta[h] * (beta[h] * (1.0 - 0.5 * beta[h])), 0.0)
        r = dirs[h][1]
        dc = r * (dw[h] - w[h] * jnp.sum(w[h] * dw[h], axis=1, keepdims=True))
        taps = taps_ref[:, cols[h]]
        dpath = dc * taps[0:1]
        dtaps = [jnp.sum(dc * path[h], axis=0, keepdims=True)]
        for s in range(1, taps.shape[0]):
            up = shift_up(jnp.where(kept(dc.shape, s, first), dc, 0.0), s)
            dpath = dpath + up * taps[s : s + 1]
            dtaps.append(jnp.sum(up * path[h], axis=0, keepdims=True))
        dvp_ref[1, :, cols[h]] = dpath.astype(bf)
        dtaps_ref[:, cols[h]] = jnp.concatenate(dtaps, axis=0)

    @pl.when(pl.program_id(0) == 0)
    def _():
        dlogit_ref[...] = out

    @pl.when(pl.program_id(0) > 0)
    def _():
        dlogit_ref[...] += out


VM = 60 * 1024 * 1024


def specs(rows, ntaps, nh):
    wide = pl.BlockSpec((rows, HB * DH), lambda n: (0, n))
    square = pl.BlockSpec((HB, rows, rows), lambda n: (n, 0, 0))
    logit = pl.BlockSpec((rows, nh), lambda n: (0, 0))
    taps = pl.BlockSpec((ntaps, HB * DH), lambda n: (0, n))
    smem = pl.BlockSpec(memory_space=pltpu.SMEM)
    return wide, square, logit, taps, smem


def mix_forward(first, q, k, v, path, logit, taps):
    rows, width = q.shape
    nh = width // DH
    wide, square, lg, tp, sm = specs(rows, taps.shape[0], nh)
    sq = jax.ShapeDtypeStruct((nh, rows, rows), bf)
    return pl.pallas_call(
        forward_kernel,
        grid=(nh // HB,),
        in_specs=[sm, wide, wide, wide, wide, lg, tp],
        out_specs=[wide, square, square, square],
        out_shape=[jax.ShapeDtypeStruct((rows, width), bf), sq, sq, sq],
        compiler_params=pltpu.CompilerParams(vmem_limit_bytes=VM),
        cost_estimate=pl.CostEstimate(flops=12000000000, bytes_accessed=6000000, transcendentals=0),
        name="mix_forward",
    )(first, q, k, v, path, logit, taps)


def mix_backward(first, q, k, v, path, logit, taps, x, m, p, do):
    rows, width = q.shape
    nh = width // DH
    wide, square, lg, tp, sm = specs(rows, taps.shape[0], nh)
    low = jax.ShapeDtypeStruct((2, rows, width), bf)
    pair = pl.BlockSpec((2, rows, HB * DH), lambda n: (0, 0, n))
    return pl.pallas_call(
        backward_kernel,
        grid=(nh // HB,),
        in_specs=[sm, wide, wide, wide, wide, lg, tp, square, square, square, wide],
        out_specs=[pair, pair, lg, tp],
        out_shape=[low, low, jax.ShapeDtypeStruct((rows, nh), f32), jax.ShapeDtypeStruct(taps.shape, f32)],
        compiler_params=pltpu.CompilerParams(vmem_limit_bytes=VM),
        cost_estimate=pl.CostEstimate(flops=9000000000, bytes_accessed=6000000, transcendentals=0),
        name="mix_backward",
    )(first, q, k, v, path, logit, taps, x, m, p, do)


def dot_trans(left, right):
    return lax.dot_general(left, right, (((1,), (1,)), ((), ())), preferred_element_type=f32)


def dot(left, right):
    return jnp.dot(left, right, preferred_element_type=f32)


def product_kernel(near, far, b0, b1, b2, b3, away_ref, keep_ref):
    total = mm(near[0], b0[0], 1, 0) + mm(near[1], b1[0], 1, 0)
    total = (total + mm(far[0], b2[0], 1, 0) + mm(far[1], b3[0], 1, 0)).astype(bf)
    half = total.shape[0] // 2
    away_ref[...] = total[:half]
    keep_ref[...] = total[half:]


def product(left, rights):
    near, far = left
    sources, rows, slots = near.shape
    rights = [right.reshape((-1, slots, right.shape[-1])) for right in rights]
    count, _, width = rights[0].shape
    tile = 512 if width % 512 == 0 else 384
    tiles = width // tile
    half = jax.ShapeDtypeStruct((rows // 2, count * width), bf)
    return pl.pallas_call(
        product_kernel,
        grid=(count, tiles),
        in_specs=[pl.BlockSpec((sources, rows, slots), lambda c, n: (0, 0, 0))] * 2
        + [pl.BlockSpec((1, slots, tile), lambda c, n: (c, 0, n))] * 4,
        out_specs=[pl.BlockSpec((rows // 2, tile), lambda c, n: (0, c * tiles + n))] * 2,
        out_shape=[half, half],
        compiler_params=pltpu.CompilerParams(vmem_limit_bytes=VM // 2),
        cost_estimate=pl.CostEstimate(
            flops=4 * 10**6 * width * count // 3, bytes_accessed=2000 * width * count, transcendentals=0
        ),
        name="product",
    )(near, far, *rights)


def turn_kernel(blocks_ref, own_ref, core_ref, near_ref, far_ref, turned):
    count = near_ref.shape[1] // blocks_ref.shape[1]
    for source, ref in enumerate((own_ref, core_ref)):
        for n in range(ref.shape[1] // DH):
            turned[n * DH : (n + 1) * DH, :] = ref[:, n * DH : (n + 1) * DH].T
        for which, out in enumerate((near_ref, far_ref)):
            for n in range(blocks_ref.shape[1]):
                start = pl.multiple_of(blocks_ref[which, n] * count, 16)
                out[source, n * count : (n + 1) * count, :] = turned[pl.ds(start, count), :]


def turn(blocks, own, core):
    slots, features = own.shape
    rows = features // 4
    out = jax.ShapeDtypeStruct((2, rows, slots), bf)
    per = rows // blocks.shape[1]
    if per % 16:
        both = jnp.stack([own.T, core.T]).reshape(2, features // per, per, slots)
        return [both[:, blocks[n]].reshape(2, rows, slots) for n in range(2)]
    vmem = pl.BlockSpec(memory_space=pltpu.VMEM)
    return pl.pallas_call(
        turn_kernel,
        in_specs=[pl.BlockSpec(memory_space=pltpu.SMEM), vmem, vmem],
        out_specs=[vmem, vmem],
        out_shape=[out, out],
        scratch_shapes=[pltpu.VMEM((features, slots), bf)],
        compiler_params=pltpu.CompilerParams(vmem_limit_bytes=VM // 2),
        cost_estimate=pl.CostEstimate(flops=0, bytes_accessed=6000000, transcendentals=0),
        name="turn",
    )(blocks, own, core)


def after(array, *others):
    return lax.optimization_barrier((array,) + others)[0]


def pick(array, which, axis=0):
    return lax.dynamic_index_in_dim(array, which, axis, keepdims=False)


class Links:
    def __init__(self):
        self.count = lax.axis_size("dp")
        self.pair_last = self.line_last = ()
        self.line = self.count // 4
        self.me = lax.axis_index("dp")
        self.core = self.me % 2
        self.pair = (self.me // 2) % 2
        self.place = self.me // 4
        places = [self.place]
        bit = self.line // 2
        while bit >= 1:
            places = [p ^ bit for p in places] + places
            bit //= 2
        chips = jnp.stack(places) * 4 + self.core
        self.blocks = jnp.stack([chips + 2 * self.pair, chips + 2 * (1 - self.pair)]).astype(jnp.int32)

    def flip(self, array, bit):
        return lax.ppermute(array, "dp", [(i, i ^ bit) for i in range(self.count)])

    def left(self, array):
        near, away = turn(self.blocks, array, self.flip(array, 1))
        return near, self.pair_rows(away)

    def pair_rows(self, array):
        self.pair_last = self.flip(after(array, *self.pair_last), 2),
        return self.pair_last[0]

    def right(self, array, theirs):
        return [array, self.flip(after(array, theirs), 1), theirs, self.flip(theirs, 1)]

    def first(self, halves):
        away, keep = halves
        bit = 1
        while 2 * bit <= self.line // 2:
            if bit == 1:
                self.line_last = self.flip(after(away, *self.line_last), 4),
                got = self.line_last[0]
            else:
                got = self.flip(away, 4 * bit)
            half = keep.shape[0] // 2
            away, keep = keep[:half] + got[:half], keep[half:] + got[half:]
            bit *= 2
        return away, keep

    def second(self, halves, *before):
        away, keep = halves
        got = self.flip(away, 2 * self.line)
        return keep.astype(f32) + after(got, *before).astype(f32)


def swap(array):
    return lax.ppermute(array, "head", [(0, 1), (1, 0)])


def in_order(own, other, place):
    return jnp.concatenate([jnp.where(place == 0, own, other), jnp.where(place == 0, other, own)], axis=0)


def norm_back(grad, values, gain, scale):
    scaled = gain * grad
    mean = jnp.mean(scaled * values, axis=1, keepdims=True)
    return scale * scaled - values * (scale * scale * scale) * mean


def norm_scale(values):
    return lax.rsqrt(jnp.mean(values * values, axis=1, keepdims=True) + 1e-6)


def per_device(
    tokens,
    norm1_gain,
    w_query,
    w_key,
    w_value,
    w_path,
    w_beta,
    conv_kernel,
    w_output,
    norm2_gain,
    w_gate,
    w_up,
    w_down,
    item_lengths,
    cotangent,
):
    links = Links()
    head = lax.axis_index("head")
    local = tokens.shape[0]
    depth = tokens.shape[1]

    tokens_other = swap(tokens)
    tokens_all = in_order(tokens, tokens_other, head)

    quarter = 2 * links.pair + links.core
    quarters = w_output.reshape(4, depth // 4, w_output.shape[1])
    got = swap(after(pick(quarters, quarter), tokens_other))
    cot_other = swap(after(cotangent, got))
    cot_all = in_order(cotangent, cot_other, head)

    inputs = tokens_all.astype(f32)
    scale1 = norm_scale(inputs)
    normed1 = (inputs * scale1 * norm1_gain).astype(bf)
    queries = dot(normed1, w_query).astype(bf)
    keys = dot(normed1, w_key).astype(bf)
    values = dot(normed1, w_value).astype(bf)
    path_raw = dot(normed1, w_path)
    beta_logit = dot(normed1, w_beta)
    taps = jnp.transpose(conv_kernel, (2, 1, 0)).reshape(conv_kernel.shape[2], -1)

    queries = after(queries, got)
    got_pair = links.pair_rows(got)
    mixed, solved, moved, probs = mix_forward(item_lengths, queries, keys, values, path_raw, beta_logit, taps)
    mixed_other = swap(after(mixed, cot_other, got_pair))
    left_one = links.left(after(normed1, mixed))
    got_core = links.flip(jnp.stack([got, got_pair]), 1)
    left_cot = links.left(after(cot_all, mixed_other))
    pairs_mixed = links.pair_rows(mixed)

    def chosen(pair, core):
        near = jnp.where(core == links.core, got, got_core[0])
        far = jnp.where(core == links.core, got_pair, got_core[1])
        return jnp.where(pair == links.pair, near, far)

    w_output_other = jnp.concatenate([chosen(0, 0), chosen(0, 1), chosen(1, 0), chosen(1, 1)], axis=0)
    resid = inputs + dot_trans(mixed, w_output) + dot_trans(mixed_other, w_output_other)
    scale2 = norm_scale(resid)
    normed2 = (resid * scale2 * norm2_gain).astype(bf)
    gate = dot(normed2, w_gate)
    upper = dot(normed2, w_up)
    sigma = jax.nn.sigmoid(gate)
    activated = gate * sigma
    gate, upper, hidden = lax.optimization_barrier((gate, upper, (activated * upper).astype(bf)))
    sigma = jax.nn.sigmoid(gate)
    activated = gate * sigma
    grad_hidden = dot(cot_all, w_down)
    grad_gate = (grad_hidden * upper * (sigma * (1.0 + gate * (1.0 - sigma)))).astype(bf)
    grad_upper = (grad_hidden * activated).astype(bf)

    middle = hidden.shape[1] // 2
    hidden_parts = [hidden[:, :middle], hidden[:, middle:]]
    pairs_down0 = links.pair_rows(hidden_parts[0])
    part2 = dot_trans(grad_gate, w_gate)
    part2 = part2 + dot_trans(after(grad_upper, pairs_down0), w_up)
    other2 = swap(part2.astype(bf))
    pairs_down1 = links.pair_rows(hidden_parts[1])
    left_two = links.left(normed2)
    product_down0 = product(left_cot, links.right(hidden_parts[0], pairs_down0))
    first_down0 = links.first(product_down0)
    product_down1 = product(left_cot, links.right(hidden_parts[1], pairs_down1))
    first_down1 = links.first(product_down1)
    pairs_gate = links.pair_rows(after(grad_gate, product_down1[0]))
    first_down = [jnp.concatenate(both, axis=1) for both in zip(first_down0, first_down1)]
    pairs_up = links.pair_rows(after(grad_upper, first_down[0]))

    other2 = after(other2, product_down1[0])
    grad_normed2 = part2 + other2.astype(f32)
    grad_gain2 = jnp.sum(grad_normed2 * resid * scale2, axis=0, keepdims=True)
    grad_resid = cot_all.astype(f32) + norm_back(grad_normed2, resid, norm2_gain, scale2)
    branch = grad_resid.astype(bf)
    grad_mixed = dot(branch, w_output).astype(bf)

    product_gate = product(left_two, links.right(grad_gate, pairs_gate))
    first_gate = links.first(product_gate)
    grad_mixed = after(grad_mixed, product_gate[0])
    grad_qk, grad_vp, grad_logit, grad_taps = mix_backward(
        item_lengths, queries, keys, values, path_raw, beta_logit, taps, solved, moved, probs, grad_mixed
    )

    def halves(array):
        return array.reshape(2, local, depth)

    low_logit = grad_logit.astype(bf)
    part = dot_trans(grad_qk[0], w_query) + dot_trans(grad_qk[1], w_key) + dot_trans(grad_vp[0], w_value)
    part = halves(part + dot_trans(grad_vp[1], w_path) + dot_trans(low_logit, w_beta))
    part_away = pick(part, 1 - head).astype(bf)
    other1 = swap(part_away)
    part_keep = pick(part, head)
    grad_w_down = links.second(first_down, part_away)
    left_branch = links.left(after(branch, part_away))
    product_up = product(left_two, links.right(grad_upper, pairs_up))
    first_up = links.first(product_up)
    grad_w_gate = links.second(first_gate, product_up[0])
    pairs_qk = links.pair_rows(after(grad_qk, product_up[0], first_gate[0]))
    product_output = product(left_branch, links.right(mixed, pairs_mixed))
    first_output = links.first(product_output)
    pairs_vp = links.pair_rows(after(grad_vp, product_output[0]))

    hidden_late = after(hidden, product_output[0])
    part = halves(dot_trans(hidden_late, w_down))
    ffn = swap(after(pick(part, 1 - head).astype(bf), other1))
    resid_own = pick(halves(resid), head)
    activations = (resid_own + pick(part, head) + ffn.astype(f32)).astype(bf)

    other1 = after(other1, product_output[0])
    grad_normed1 = part_keep + other1.astype(f32)
    inputs_own = tokens.astype(f32)
    scale_own = norm_scale(inputs_own)
    grad_tokens = pick(halves(grad_resid), head) + norm_back(grad_normed1, inputs_own, norm1_gain, scale_own)
    grad_gain1 = jnp.sum(grad_normed1 * inputs_own * scale_own, axis=0, keepdims=True)

    product_qk = product(left_one, links.right(grad_qk, pairs_qk))
    first_qk = links.first(product_qk)
    grad_w_up = links.second(first_up, product_qk[0])
    product_vp = product(left_one, links.right(grad_vp, pairs_vp))
    first_vp = links.first(product_vp)
    grad_w_output = links.second(first_output, product_vp[0])
    sum_qk = links.second(first_qk)
    sum_vp = links.second(first_vp)

    width = w_query.shape[1]
    small = lax.dot_general(low_logit, normed1, (((0,), (0,)), ((), ())), preferred_element_type=f32)
    grad_gain1 = grad_gain1 + swap(grad_gain1)
    small = jnp.concatenate([small, grad_gain1, grad_gain2], axis=0)
    heads = w_beta.shape[1]
    rows = depth // links.count
    conv_rows = conv_kernel.shape[0] // links.count
    small = jnp.swapaxes(small.reshape(-1, links.count, rows), 0, 1)
    conv = jnp.swapaxes(grad_taps.reshape(-1, links.count, conv_rows), 0, 1).reshape(links.count, 2, rows)
    small = jnp.concatenate([small, conv], axis=1)
    small = jnp.pad(small, ((0, 0), (0, 16 - small.shape[1]), (0, DH - rows))).reshape(-1, DH)
    small = lax.psum_scatter(small, "dp", scatter_dimension=0, tiled=True)
    small = after(small, links.line_last[0])[:, :rows]
    grad_w_beta = small[:heads].T
    piece = rows // 2
    gains = lax.dynamic_slice_in_dim(small[heads : heads + 2], piece * head, piece, 1)
    conv = small[heads + 2 : heads + 4].reshape(-1, heads, conv_rows)
    grad_conv = jnp.transpose(conv, (2, 1, 0))

    grad_gain1, grad_gain2 = gains[0], gains[1]
    grad_w_query, grad_w_key = sum_qk[:, :width], sum_qk[:, width:]
    grad_w_value, grad_w_path = sum_vp[:, :width], sum_vp[:, width:]
    return (
        activations,
        grad_tokens,
        grad_gain1,
        grad_w_query,
        grad_w_key,
        grad_w_value,
        grad_w_path,
        grad_w_beta,
        grad_conv,
        grad_w_output,
        grad_gain2,
        grad_w_gate,
        grad_w_up,
        grad_w_down,
    )


def solution(mesh):
    in_specs = (
        P(("dp", "head"), None),
        P(),
        P(None, "head"),
        P(None, "head"),
        P(None, "head"),
        P(None, "head"),
        P(None, "head"),
        P(None, "head", None),
        P(None, "head"),
        P(),
        P(None, "head"),
        P(None, "head"),
        P(None, "head"),
        P("dp"),
        P(("dp", "head"), None),
    )
    out_specs = (
        P(("dp", "head"), None),
        P(("dp", "head"), None),
        P(("dp", "head")),
        P("dp", "head"),
        P("dp", "head"),
        P("dp", "head"),
        P("dp", "head"),
        P("dp", "head"),
        P("dp", "head", None),
        P("dp", "head"),
        P(("dp", "head")),
        P("dp", "head"),
        P("dp", "head"),
        P("dp", "head"),
    )
    return jax.shard_map(
        per_device, mesh=mesh, in_specs=in_specs, out_specs=out_specs, check_vma=False
    )
```

```python
import jax
import jax.numpy as jnp
from jax import lax
from jax.experimental import pallas as pl
from jax.experimental.pallas import tpu as pltpu
from jax.sharding import PartitionSpec as P

f32 = jnp.float32
bf = jnp.bfloat16
DH = 128
HB = 3


def mm(a, b, ca, cb):
    return lax.dot_general(a, b, (((ca,), (cb,)), ((), ())), preferred_element_type=f32)


def parts(a):
    high = a.astype(bf)
    return high, (a - high.astype(f32)).astype(bf)


def mm3(a, b, ca, cb):
    (ah, al), (bh, bl) = a, b
    return mm(ah, bh, ca, cb) + mm(ah, bl, ca, cb) + mm(al, bh, ca, cb)


def mm2(a, b, ca, cb):
    return mm(a, b[0], ca, cb) + mm(a, b[1], ca, cb)


def index(shape):
    return lax.broadcasted_iota(jnp.int32, shape, 0), lax.broadcasted_iota(jnp.int32, shape, 1)


def column(array, which):
    lane = lax.broadcasted_iota(jnp.int32, array.shape, 1)
    return jnp.sum(jnp.where(lane == which, array, 0.0), axis=1, keepdims=True)


def shift_down(a, s):
    return jnp.concatenate([jnp.zeros((s, a.shape[1]), a.dtype), a[: a.shape[0] - s]], axis=0)


def shift_up(a, s):
    return jnp.concatenate([a[s:], jnp.zeros((s, a.shape[1]), a.dtype)], axis=0)


def kept(shape, s, first):
    t = lax.broadcasted_iota(jnp.int32, shape, 0)
    return (t >= s) & ~((t >= first) & (t - s < first))


def directions(path, taps, first):
    total = path * taps[0:1]
    for s in range(1, taps.shape[0]):
        total = total + jnp.where(kept(path.shape, s, first), shift_down(path, s), 0.0) * taps[s : s + 1]
    r = lax.rsqrt(jnp.sum(total * total, axis=1, keepdims=True) + 1e-6)
    return total * r, r


def inverses(systems):
    size = systems[0].shape[0]
    i, j = index((size, size))
    solved = [jnp.where(i == j, 1.0, 0.0) - jnp.where(i // 2 == j // 2, a, 0.0) for a in systems]
    width = 2
    while width < size:
        inside = (i // (2 * width) == j // (2 * width)) & (i // width != j // width)
        offs = [parts(jnp.where(inside, a, 0.0)) for a in systems]
        lows = [parts(x) for x in solved]
        inner = [parts(mm3(o, x, 1, 0)) for o, x in zip(offs, lows)]
        solved = [x - mm3(l, y, 1, 0) for x, l, y in zip(solved, lows, inner)]
        width *= 2
    return solved


def forward_kernel(first_ref, q_ref, k_ref, v_ref, path_ref, logit_ref, taps_ref, o_ref, x_ref, m_ref, p_ref):
    first = first_ref[0]
    rows = q_ref.shape[0]
    half = rows // 2
    base = pl.program_id(0) * HB
    heads = range(HB)
    cols = [slice(h * DH, (h + 1) * DH) for h in heads]
    i, j = index((rows, rows))
    q = [q_ref[:, c] for c in cols]
    k = [k_ref[:, c] for c in cols]
    w = [parts(directions(path_ref[:, c], taps_ref[:, c], first)[0]) for c in cols]
    logits = logit_ref[...]
    beta = [2.0 * jax.nn.sigmoid(column(logits, base + h)) for h in heads]
    system = [jnp.where(i > j, beta[h] * mm3(w[h], w[h], 1, 1), 0.0) for h in heads]
    corners = inverses([s[:half, :half] for s in system] + [s[half:, half:] for s in system])
    corners = [parts(x) for x in corners]
    low = [parts(mm3(parts(system[h][half:, :half]), corners[h], 1, 0)) for h in heads]
    low = [parts(-mm3(corners[HB + h], low[h], 1, 0)) for h in heads]
    zero = jnp.zeros((half, half), bf)
    x = [
        tuple(
            jnp.concatenate(
                [
                    jnp.concatenate([corners[h][n], zero], axis=1),
                    jnp.concatenate([low[h][n], corners[HB + h][n]], axis=1),
                ],
                axis=0,
            )
            for n in range(2)
        )
        for h in heads
    ]
    qw = [parts(jnp.where(i >= j, mm2(q[h], w[h], 1, 1), 0.0)) for h in heads]
    wk = [mm(w[h][0], k[h], 1, 1) + mm(w[h][1], k[h], 1, 1) for h in heads]
    wk = [parts(jnp.where(i > j, beta[h] * wk[h], 0.0)) for h in heads]
    m = [parts(mm3(qw[h], x[h], 1, 0)) for h in heads]
    s = [mm(q[h], k[h], 1, 1) - mm3(m[h], wk[h], 1, 0) for h in heads]
    allowed = (i >= j) & ((i < first) | (j >= first))
    s = [jnp.where(allowed, a * DH**-0.5, -1e30) for a in s]
    e = [jnp.exp(a - jnp.max(a, axis=1, keepdims=True)) for a in s]
    p = [(a / jnp.sum(a, axis=1, keepdims=True)).astype(bf) for a in e]
    for h in heads:
        o_ref[:, cols[h]] = mm(p[h], v_ref[:, cols[h]], 1, 0).astype(bf)
        x_ref[h] = x[h][0]
        m_ref[h] = m[h][0]
        p_ref[h] = p[h]


def backward_kernel(
    first_ref, q_ref, k_ref, v_ref, path_ref, logit_ref, taps_ref, x_ref, m_ref, p_ref, do_ref,
    dqk_ref, dvp_ref, dlogit_ref, dtaps_ref,
):
    first = first_ref[0]
    rows = q_ref.shape[0]
    base = pl.program_id(0) * HB
    heads = range(HB)
    cols = [slice(h * DH, (h + 1) * DH) for h in heads]
    i, j = index((rows, rows))
    allowed = (i >= j) & ((i < first) | (j >= first))
    q = [q_ref[:, c] for c in cols]
    k = [k_ref[:, c] for c in cols]
    do = [do_ref[:, c].astype(bf) for c in cols]
    path = [path_ref[:, c] for c in cols]
    dirs = [directions(path[h], taps_ref[:, cols[h]], first) for h in heads]
    w = [d[0] for d in dirs]
    wb = [a.astype(bf) for a in w]
    logits = logit_ref[...]
    beta = [2.0 * jax.nn.sigmoid(column(logits, base + h)) for h in heads]
    p = [p_ref[h] for h in heads]
    x = [x_ref[h] for h in heads]
    m = [m_ref[h] for h in heads]
    dp = [mm(do[h], v_ref[:, cols[h]], 1, 1) for h in heads]
    for h in heads:
        dvp_ref[0, :, cols[h]] = mm(p[h], do[h], 0, 0).astype(bf)
    p = [a.astype(f32) for a in p]
    sums = [jnp.sum(dp[h] * p[h], axis=1, keepdims=True) for h in heads]
    ds = [jnp.where(allowed, p[h] * (dp[h] - sums[h]) * DH**-0.5, 0.0).astype(bf) for h in heads]
    wk = [jnp.where(i > j, mm(wb[h], k[h], 1, 1), 0.0) for h in heads]
    gram = [mm(wb[h], wb[h], 1, 1) for h in heads]
    dm = [(-mm(ds[h], (beta[h] * wk[h]).astype(bf), 1, 1)).astype(bf) for h in heads]
    dwk = [jnp.where(i > j, -mm(m[h], ds[h], 0, 0), 0.0) for h in heads]
    z = [mm(dm[h], x[h], 1, 1) for h in heads]
    dbeta = [jnp.sum(dwk[h] * wk[h], axis=1, keepdims=True) for h in heads]
    dwk = [(beta[h] * dwk[h]).astype(bf) for h in heads]
    da = [jnp.where(i > j, -mm(m[h], z[h].astype(bf), 0, 0), 0.0) for h in heads]
    dqw = [jnp.where(i >= j, z[h], 0.0).astype(bf) for h in heads]
    dbeta = [dbeta[h] + jnp.sum(da[h] * gram[h], axis=1, keepdims=True) for h in heads]
    dg = [(beta[h] * da[h]).astype(bf) for h in heads]
    dw = [mm(dg[h], wb[h], 1, 0) + mm(dg[h], wb[h], 0, 0) + mm(dqw[h], q[h], 0, 0) + mm(dwk[h], k[h], 1, 0) for h in heads]
    for h in heads:
        dqk_ref[0, :, cols[h]] = (mm(ds[h], k[h], 1, 0) + mm(dqw[h], wb[h], 1, 0)).astype(bf)
        dqk_ref[1, :, cols[h]] = (mm(ds[h], q[h], 0, 0) + mm(dwk[h], wb[h], 0, 0)).astype(bf)
    lane = lax.broadcasted_iota(jnp.int32, logits.shape, 1)
    out = jnp.zeros_like(logits)
    for h in heads:
        out = out + jnp.where(lane == base + h, dbeta[h] * (beta[h] * (1.0 - 0.5 * beta[h])), 0.0)
        r = dirs[h][1]
        dc = r * (dw[h] - w[h] * jnp.sum(w[h] * dw[h], axis=1, keepdims=True))
        taps = taps_ref[:, cols[h]]
        dpath = dc * taps[0:1]
        dtaps = [jnp.sum(dc * path[h], axis=0, keepdims=True)]
        for s in range(1, taps.shape[0]):
            up = shift_up(jnp.where(kept(dc.shape, s, first), dc, 0.0), s)
            dpath = dpath + up * taps[s : s + 1]
            dtaps.append(jnp.sum(up * path[h], axis=0, keepdims=True))
        dvp_ref[1, :, cols[h]] = dpath.astype(bf)
        dtaps_ref[:, cols[h]] = jnp.concatenate(dtaps, axis=0)

    @pl.when(pl.program_id(0) == 0)
    def _():
        dlogit_ref[...] = out

    @pl.when(pl.program_id(0) > 0)
    def _():
        dlogit_ref[...] += out


VM = 60 * 1024 * 1024


def specs(rows, ntaps, nh):
    wide = pl.BlockSpec((rows, HB * DH), lambda n: (0, n))
    square = pl.BlockSpec((HB, rows, rows), lambda n: (n, 0, 0))
    logit = pl.BlockSpec((rows, nh), lambda n: (0, 0))
    taps = pl.BlockSpec((ntaps, HB * DH), lambda n: (0, n))
    smem = pl.BlockSpec(memory_space=pltpu.SMEM)
    return wide, square, logit, taps, smem


def mix_forward(first, q, k, v, path, logit, taps):
    rows, width = q.shape
    nh = width // DH
    wide, square, lg, tp, sm = specs(rows, taps.shape[0], nh)
    sq = jax.ShapeDtypeStruct((nh, rows, rows), bf)
    return pl.pallas_call(
        forward_kernel,
        grid=(nh // HB,),
        in_specs=[sm, wide, wide, wide, wide, lg, tp],
        out_specs=[wide, square, square, square],
        out_shape=[jax.ShapeDtypeStruct((rows, width), bf), sq, sq, sq],
        compiler_params=pltpu.CompilerParams(vmem_limit_bytes=VM),
        cost_estimate=pl.CostEstimate(flops=12000000000, bytes_accessed=6000000, transcendentals=0),
        name="mix_forward",
    )(first, q, k, v, path, logit, taps)


def mix_backward(first, q, k, v, path, logit, taps, x, m, p, do):
    rows, width = q.shape
    nh = width // DH
    wide, square, lg, tp, sm = specs(rows, taps.shape[0], nh)
    low = jax.ShapeDtypeStruct((2, rows, width), bf)
    pair = pl.BlockSpec((2, rows, HB * DH), lambda n: (0, 0, n))
    return pl.pallas_call(
        backward_kernel,
        grid=(nh // HB,),
        in_specs=[sm, wide, wide, wide, wide, lg, tp, square, square, square, wide],
        out_specs=[pair, pair, lg, tp],
        out_shape=[low, low, jax.ShapeDtypeStruct((rows, nh), f32), jax.ShapeDtypeStruct(taps.shape, f32)],
        compiler_params=pltpu.CompilerParams(vmem_limit_bytes=VM),
        cost_estimate=pl.CostEstimate(flops=9000000000, bytes_accessed=6000000, transcendentals=0),
        name="mix_backward",
    )(first, q, k, v, path, logit, taps, x, m, p, do)


def dot_trans(left, right):
    return lax.dot_general(left, right, (((1,), (1,)), ((), ())), preferred_element_type=f32)


def dot(left, right):
    return jnp.dot(left, right, preferred_element_type=f32)


def product_kernel(near, far, b0, b1, away_ref, keep_ref):
    total = (mm(near[...], b0[0], 1, 0) + mm(far[...], b1[0], 1, 0)).astype(bf)
    half = total.shape[0] // 2
    away_ref[...] = total[:half]
    keep_ref[...] = total[half:]


def product(left, rights):
    near, far = left
    rows, slots = near.shape
    rights = [right.reshape((-1, slots, right.shape[-1])) for right in rights]
    count, _, width = rights[0].shape
    tile = 512 if width % 512 == 0 else 384
    tiles = width // tile
    half = jax.ShapeDtypeStruct((rows // 2, count * width), bf)
    return pl.pallas_call(
        product_kernel,
        grid=(count, tiles),
        in_specs=[pl.BlockSpec((rows, slots), lambda c, n: (0, 0))] * 2
        + [pl.BlockSpec((1, slots, tile), lambda c, n: (c, 0, n))] * 2,
        out_specs=[pl.BlockSpec((rows // 2, tile), lambda c, n: (0, c * tiles + n))] * 2,
        out_shape=[half, half],
        compiler_params=pltpu.CompilerParams(vmem_limit_bytes=VM // 2),
        cost_estimate=pl.CostEstimate(
            flops=4 * 10**6 * width * count // 3, bytes_accessed=2000 * width * count, transcendentals=0
        ),
        name="product",
    )(near, far, *rights)


def turn_kernel(blocks_ref, own_ref, near_ref, far_ref, turned):
    count = near_ref.shape[0] // blocks_ref.shape[1]
    for n in range(own_ref.shape[1] // DH):
        turned[n * DH : (n + 1) * DH, :] = own_ref[:, n * DH : (n + 1) * DH].T
    for which, out in enumerate((near_ref, far_ref)):
        for n in range(blocks_ref.shape[1]):
            start = pl.multiple_of(blocks_ref[which, n] * count, 16)
            out[n * count : (n + 1) * count, :] = turned[pl.ds(start, count), :]


def turn(blocks, own):
    slots, features = own.shape
    rows = features // 2
    out = jax.ShapeDtypeStruct((rows, slots), bf)
    per = rows // blocks.shape[1]
    if per % 16:
        turned = own.T.reshape(features // per, per, slots)
        return [turned[blocks[n]].reshape(rows, slots) for n in range(2)]
    vmem = pl.BlockSpec(memory_space=pltpu.VMEM)
    return pl.pallas_call(
        turn_kernel,
        in_specs=[pl.BlockSpec(memory_space=pltpu.SMEM), vmem],
        out_specs=[vmem, vmem],
        out_shape=[out, out],
        scratch_shapes=[pltpu.VMEM((features, slots), bf)],
        compiler_params=pltpu.CompilerParams(vmem_limit_bytes=VM // 2),
        cost_estimate=pl.CostEstimate(flops=0, bytes_accessed=4 * slots * features, transcendentals=0),
        name="turn",
    )(blocks, own)


def back_kernel(first, second, w0, w1, w2, w3, o_ref):
    total = mm(first[0], w0[...], 1, 1) + mm(first[1], w1[...], 1, 1)
    o_ref[...] = total + mm(second[0], w2[...], 1, 1) + mm(second[1], w3[...], 1, 1)


def back(first, second, weights):
    _, slots, width = first.shape
    depth = weights[0].shape[0]
    tile = 512 if depth % 512 == 0 else DH
    return pl.pallas_call(
        back_kernel,
        grid=(depth // tile,),
        in_specs=[pl.BlockSpec((2, slots, width), lambda n: (0, 0, 0))] * 2
        + [pl.BlockSpec((tile, width), lambda n: (n, 0))] * 4,
        out_specs=pl.BlockSpec((slots, tile), lambda n: (0, n)),
        out_shape=jax.ShapeDtypeStruct((slots, depth), f32),
        compiler_params=pltpu.CompilerParams(vmem_limit_bytes=VM // 2),
        cost_estimate=pl.CostEstimate(flops=5 * 10**9, bytes_accessed=11 * 10**6, transcendentals=0),
        name="back",
    )(first, second, *weights)


def after(array, *others):
    return lax.optimization_barrier((array,) + others)[0]


def pick(array, which, axis=0):
    return lax.dynamic_index_in_dim(array, which, axis, keepdims=False)


class Links:
    def __init__(self):
        self.count = lax.axis_size("dp")
        self.pair_last = ()
        self.line = self.count // 4
        self.me = lax.axis_index("dp")
        self.core = self.me % 2
        self.pair = (self.me // 2) % 2
        self.place = self.me // 4
        places = [self.place]
        bit = self.line // 2
        while bit >= 1:
            places = [p ^ bit for p in places] + places
            bit //= 2

        def listed(places):
            chips = [
                jnp.concatenate([4 * places + 2 * pair + 1 - self.core, 4 * places + 2 * pair + self.core])
                for pair in (self.pair, 1 - self.pair)
            ]
            return jnp.stack(chips).astype(jnp.int32)

        self.halving = listed(jnp.stack(places))
        self.in_line = listed(jnp.arange(self.line, dtype=jnp.int32))
        self.lines = [[4 * place + n for place in range(self.line)] for n in range(4)]

    def flip(self, array, bit):
        return lax.ppermute(array, "dp", [(i, i ^ bit) for i in range(self.count)])

    def left(self, array, blocks):
        near, away = turn(blocks, array)
        return near, self.pair_rows(away)

    def pair_rows(self, array, together=1):
        got = self.flip(after(array, *self.pair_last[: 3 - together]), 2)
        self.pair_last = self.pair_last[-1:] + (got,)
        return got

    def chosen(self, array):
        own = self.halving[0, self.line :]
        return jnp.concatenate([pick(array, own[n]) for n in range(self.line)], axis=0)

    def cores(self, halves):
        away, keep = halves
        return keep + self.flip(away, 1)

    def scatter(self, partial):
        return lax.psum_scatter(
            partial, "dp", scatter_dimension=0, axis_index_groups=self.lines, tiled=True
        ).astype(f32)

    def first(self, total):
        half = total.shape[0] // 2
        away, keep = total[:half], total[half:]
        bit = 1
        while 2 * bit <= self.line // 2:
            got = self.flip(away, 4 * bit)
            half = keep.shape[0] // 2
            away, keep = keep[:half] + got[:half], keep[half:] + got[half:]
            bit *= 2
        return away, keep

    def second(self, halves, *before):
        away, keep = halves
        got = self.flip(away, 2 * self.line)
        return keep.astype(f32) + after(got, *before).astype(f32)


def swap(array):
    return lax.ppermute(array, "head", [(0, 1), (1, 0)])


def in_order(own, other, place):
    return jnp.concatenate([jnp.where(place == 0, own, other), jnp.where(place == 0, other, own)], axis=0)


def norm_back(grad, values, gain, scale):
    scaled = gain * grad
    mean = jnp.mean(scaled * values, axis=1, keepdims=True)
    return scale * scaled - values * (scale * scale * scale) * mean


def norm_scale(values):
    return lax.rsqrt(jnp.mean(values * values, axis=1, keepdims=True) + 1e-6)


def per_device(
    tokens,
    norm1_gain,
    w_query,
    w_key,
    w_value,
    w_path,
    w_beta,
    conv_kernel,
    w_output,
    norm2_gain,
    w_gate,
    w_up,
    w_down,
    item_lengths,
    cotangent,
):
    links = Links()
    head = lax.axis_index("head")
    local = tokens.shape[0]
    depth = tokens.shape[1]

    tokens_other = swap(tokens)
    tokens_all = in_order(tokens, tokens_other, head)

    quarter = 2 * links.pair + links.core
    quarters = w_output.reshape(4, depth // 4, w_output.shape[1])
    got = swap(after(pick(quarters, quarter), tokens_other))
    cot_other = swap(after(cotangent, got))
    cot_all = in_order(cotangent, cot_other, head)

    inputs = tokens_all.astype(f32)
    scale1 = norm_scale(inputs)
    normed1 = (inputs * scale1 * norm1_gain).astype(bf)
    queries = dot(normed1, w_query).astype(bf)
    keys = dot(normed1, w_key).astype(bf)
    values = dot(normed1, w_value).astype(bf)
    path_raw = dot(normed1, w_path)
    beta_logit = dot(normed1, w_beta)
    taps = jnp.transpose(conv_kernel, (2, 1, 0)).reshape(conv_kernel.shape[2], -1)

    queries = after(queries, got)
    got_pair = links.pair_rows(got)
    mixed, solved, moved, probs = mix_forward(item_lengths, queries, keys, values, path_raw, beta_logit, taps)
    mixed_other = swap(after(mixed, cot_other, got_pair))
    got_core = links.flip(jnp.stack([got, after(got_pair, mixed)]), 1)
    left_cot = links.left(after(cot_all, mixed), links.in_line)

    def chosen(pair, core):
        near = jnp.where(core == links.core, got, got_core[0])
        far = jnp.where(core == links.core, got_pair, got_core[1])
        return jnp.where(pair == links.pair, near, far)

    w_output_other = jnp.concatenate([chosen(0, 0), chosen(0, 1), chosen(1, 0), chosen(1, 1)], axis=0)
    near_one, far_one = turn(links.halving, normed1)
    mixed_other = after(mixed_other, near_one)
    resid = inputs + dot_trans(mixed, w_output) + dot_trans(mixed_other, w_output_other)
    scale2 = norm_scale(resid)
    normed2 = (resid * scale2 * norm2_gain).astype(bf)
    near_two, far_two = turn(links.in_line, normed2)
    gate = dot(normed2, w_gate)
    upper = dot(normed2, w_up)
    sigma = jax.nn.sigmoid(gate)
    activated = gate * sigma
    gate, upper, hidden = lax.optimization_barrier((gate, upper, (activated * upper).astype(bf)))
    sigma = jax.nn.sigmoid(gate)
    activated = gate * sigma
    grad_hidden = dot(cot_all, w_down)
    grad_gate = (grad_hidden * upper * (sigma * (1.0 + gate * (1.0 - sigma)))).astype(bf)
    grad_upper = (grad_hidden * activated).astype(bf)

    pairs_hidden = links.pair_rows(after(hidden, near_two))
    part2 = dot_trans(grad_gate, w_gate) + dot_trans(grad_upper, w_up)
    other2 = swap(part2.astype(bf))
    total_down = links.cores(product(left_cot, (after(hidden, other2), pairs_hidden)))
    grad_w_down = links.scatter(total_down)
    pairs_gate = links.pair_rows(grad_gate)

    other2 = after(other2, total_down)
    grad_normed2 = part2 + other2.astype(f32)
    grad_gain2 = jnp.sum(grad_normed2 * resid * scale2, axis=0, keepdims=True)
    grad_resid = cot_all.astype(f32) + norm_back(grad_normed2, resid, norm2_gain, scale2)
    branch = grad_resid.astype(bf)
    grad_mixed = dot(branch, w_output).astype(bf)
    grad_qk, grad_vp, grad_logit, grad_taps = mix_backward(
        item_lengths, queries, keys, values, path_raw, beta_logit, taps, solved, moved, probs, grad_mixed
    )

    def halves(array):
        return array.reshape(2, local, depth)

    left_two = near_two, links.pair_rows(after(far_two, grad_qk))
    pairs_up = links.pair_rows(grad_upper)
    near_branch, far_branch = turn(links.halving, after(branch, grad_qk))
    left_one = near_one, links.pair_rows(far_one)
    product_gate = product(left_two, (after(grad_gate, grad_qk), pairs_gate))
    total_gate = links.cores(product_gate)
    grad_w_gate = links.scatter(total_gate)
    low_logit = grad_logit.astype(bf)
    part = back(after(grad_qk, total_gate, near_branch, grad_w_down), grad_vp, (w_query, w_key, w_value, w_path))
    part = halves(part + dot_trans(low_logit, w_beta))
    part_away = pick(part, 1 - head).astype(bf)
    other1 = swap(part_away)
    part_keep = pick(part, head)
    total_up = links.cores(product(left_two, (after(grad_upper, part_away), pairs_up)))
    grad_w_up = links.scatter(total_up)
    pairs_qk = links.pair_rows(grad_qk)
    other1 = after(other1, total_up)
    grad_normed1 = part_keep + other1.astype(f32)
    inputs_own = tokens.astype(f32)
    scale_own = norm_scale(inputs_own)
    grad_tokens = pick(halves(grad_resid), head) + norm_back(grad_normed1, inputs_own, norm1_gain, scale_own)
    grad_gain1 = jnp.sum(grad_normed1 * inputs_own * scale_own, axis=0, keepdims=True)

    width = w_query.shape[1]
    low_logit, grad_gain2 = after(low_logit, total_up), after(grad_gain2, total_up)
    grad_taps = after(grad_taps, total_up)
    small = lax.dot_general(low_logit, normed1, (((0,), (0,)), ((), ())), preferred_element_type=f32)
    grad_gain1 = grad_gain1 + swap(grad_gain1)
    small = jnp.concatenate([small, grad_gain1, grad_gain2], axis=0)
    heads = w_beta.shape[1]
    rows = depth // links.count
    conv_rows = conv_kernel.shape[0] // links.count
    small = jnp.swapaxes(small.reshape(-1, links.count, rows), 0, 1)
    conv = jnp.swapaxes(grad_taps.reshape(-1, links.count, conv_rows), 0, 1).reshape(links.count, 2, rows)
    small = jnp.concatenate([small, conv], axis=1)
    small = jnp.pad(small, ((0, 0), (0, 16 - small.shape[1]), (0, DH - rows)))

    left_branch = near_branch, links.pair_rows(after(far_branch, total_up, small))
    pairs_vp = links.pair_rows(grad_vp)
    pairs_mixed = links.pair_rows(mixed, 2)
    total_qk = links.cores(product(left_one, (after(grad_qk, grad_w_gate, small), pairs_qk)))
    first_qk = links.first(total_qk)
    total_vp = links.cores(product(left_one, (after(grad_vp, grad_w_up, first_qk[0]), pairs_vp)))
    first_vp = links.first(total_vp)
    hidden_late = after(hidden, total_vp)
    part = halves(dot_trans(hidden_late, w_down))
    ffn_away = pick(part, 1 - head).astype(bf)
    ffn = swap(after(ffn_away, other1))
    resid_own = pick(halves(resid), head)
    activations = (resid_own + pick(part, head) + ffn.astype(f32)).astype(bf)
    sum_qk = links.second(first_qk)
    total_output = links.cores(product(left_branch, (after(mixed, total_vp), pairs_mixed)))
    first_output = links.first(total_output)
    sum_vp = links.second(first_vp)
    grad_w_output = links.second(first_output)
    core_small = small + links.flip(small, 1)
    pair_small = core_small + links.pair_rows(after(core_small, total_vp))
    small = links.second(links.first(links.chosen(pair_small)))[:, :rows]

    width = w_query.shape[1]
    grad_w_beta = small[:heads].T
    piece = rows // 2
    gains = lax.dynamic_slice_in_dim(small[heads : heads + 2], piece * head, piece, 1)
    conv = small[heads + 2 : heads + 4].reshape(-1, heads, conv_rows)
    grad_conv = jnp.transpose(conv, (2, 1, 0))

    grad_gain1, grad_gain2 = gains[0], gains[1]
    grad_w_query, grad_w_key = sum_qk[:, :width], sum_qk[:, width:]
    grad_w_value, grad_w_path = sum_vp[:, :width], sum_vp[:, width:]
    return (
        activations,
        grad_tokens,
        grad_gain1,
        grad_w_query,
        grad_w_key,
        grad_w_value,
        grad_w_path,
        grad_w_beta,
        grad_conv,
        grad_w_output,
        grad_gain2,
        grad_w_gate,
        grad_w_up,
        grad_w_down,
    )


def solution(mesh):
    in_specs = (
        P(("dp", "head"), None),
        P(),
        P(None, "head"),
        P(None, "head"),
        P(None, "head"),
        P(None, "head"),
        P(None, "head"),
        P(None, "head", None),
        P(None, "head"),
        P(),
        P(None, "head"),
        P(None, "head"),
        P(None, "head"),
        P("dp"),
        P(("dp", "head"), None),
    )
    out_specs = (
        P(("dp", "head"), None),
        P(("dp", "head"), None),
        P(("dp", "head")),
        P("dp", "head"),
        P("dp", "head"),
        P("dp", "head"),
        P("dp", "head"),
        P("dp", "head"),
        P("dp", "head", None),
        P("dp", "head"),
        P(("dp", "head")),
        P("dp", "head"),
        P("dp", "head"),
        P("dp", "head"),
    )
    return jax.shard_map(
        per_device, mesh=mesh, in_specs=in_specs, out_specs=out_specs, check_vma=False
    )
```

```python
import jax
import jax.numpy as jnp
from jax import lax
from jax.experimental import pallas as pl
from jax.experimental.pallas import tpu as pltpu
from jax.sharding import PartitionSpec as P

f32 = jnp.float32
bf = jnp.bfloat16
DH = 128
HB = 3


def mm(a, b, ca, cb):
    return lax.dot_general(a, b, (((ca,), (cb,)), ((), ())), preferred_element_type=f32)


def parts(a):
    high = a.astype(bf)
    return high, (a - high.astype(f32)).astype(bf)


def mm3(a, b, ca, cb):
    (ah, al), (bh, bl) = a, b
    return mm(ah, bh, ca, cb) + mm(ah, bl, ca, cb) + mm(al, bh, ca, cb)


def mm2(a, b, ca, cb):
    return mm(a, b[0], ca, cb) + mm(a, b[1], ca, cb)


def index(shape):
    return lax.broadcasted_iota(jnp.int32, shape, 0), lax.broadcasted_iota(jnp.int32, shape, 1)


def column(array, which):
    lane = lax.broadcasted_iota(jnp.int32, array.shape, 1)
    return jnp.sum(jnp.where(lane == which, array, 0.0), axis=1, keepdims=True)


def shift_down(a, s):
    return jnp.concatenate([jnp.zeros((s, a.shape[1]), a.dtype), a[: a.shape[0] - s]], axis=0)


def shift_up(a, s):
    return jnp.concatenate([a[s:], jnp.zeros((s, a.shape[1]), a.dtype)], axis=0)


def kept(shape, s, first):
    t = lax.broadcasted_iota(jnp.int32, shape, 0)
    return (t >= s) & ~((t >= first) & (t - s < first))


def directions(path, taps, first):
    total = path * taps[0:1]
    for s in range(1, taps.shape[0]):
        total = total + jnp.where(kept(path.shape, s, first), shift_down(path, s), 0.0) * taps[s : s + 1]
    r = lax.rsqrt(jnp.sum(total * total, axis=1, keepdims=True) + 1e-6)
    return total * r, r


def inverses(systems):
    size = systems[0].shape[0]
    i, j = index((size, size))
    solved = [jnp.where(i == j, 1.0, 0.0) - jnp.where(i // 2 == j // 2, a, 0.0) for a in systems]
    width = 2
    while width < size:
        inside = (i // (2 * width) == j // (2 * width)) & (i // width != j // width)
        offs = [parts(jnp.where(inside, a, 0.0)) for a in systems]
        lows = [parts(x) for x in solved]
        inner = [parts(mm3(o, x, 1, 0)) for o, x in zip(offs, lows)]
        solved = [x - mm3(l, y, 1, 0) for x, l, y in zip(solved, lows, inner)]
        width *= 2
    return solved


def forward_kernel(first_ref, q_ref, k_ref, v_ref, path_ref, logit_ref, taps_ref, o_ref, x_ref, m_ref, p_ref):
    first = first_ref[0]
    rows = q_ref.shape[0]
    half = rows // 2
    base = pl.program_id(0) * HB
    heads = range(HB)
    cols = [slice(h * DH, (h + 1) * DH) for h in heads]
    i, j = index((rows, rows))
    q = [q_ref[:, c] for c in cols]
    k = [k_ref[:, c] for c in cols]
    w = [parts(directions(path_ref[:, c], taps_ref[:, c], first)[0]) for c in cols]
    logits = logit_ref[...]
    beta = [2.0 * jax.nn.sigmoid(column(logits, base + h)) for h in heads]
    system = [jnp.where(i > j, beta[h] * mm3(w[h], w[h], 1, 1), 0.0) for h in heads]
    corners = inverses([s[:half, :half] for s in system] + [s[half:, half:] for s in system])
    corners = [parts(x) for x in corners]
    low = [parts(mm3(parts(system[h][half:, :half]), corners[h], 1, 0)) for h in heads]
    low = [parts(-mm3(corners[HB + h], low[h], 1, 0)) for h in heads]
    zero = jnp.zeros((half, half), bf)
    x = [
        tuple(
            jnp.concatenate(
                [
                    jnp.concatenate([corners[h][n], zero], axis=1),
                    jnp.concatenate([low[h][n], corners[HB + h][n]], axis=1),
                ],
                axis=0,
            )
            for n in range(2)
        )
        for h in heads
    ]
    qw = [parts(jnp.where(i >= j, mm2(q[h], w[h], 1, 1), 0.0)) for h in heads]
    wk = [mm(w[h][0], k[h], 1, 1) + mm(w[h][1], k[h], 1, 1) for h in heads]
    wk = [parts(jnp.where(i > j, beta[h] * wk[h], 0.0)) for h in heads]
    m = [parts(mm3(qw[h], x[h], 1, 0)) for h in heads]
    s = [mm(q[h], k[h], 1, 1) - mm3(m[h], wk[h], 1, 0) for h in heads]
    allowed = (i >= j) & ((i < first) | (j >= first))
    s = [jnp.where(allowed, a * DH**-0.5, -1e30) for a in s]
    e = [jnp.exp(a - jnp.max(a, axis=1, keepdims=True)) for a in s]
    p = [(a / jnp.sum(a, axis=1, keepdims=True)).astype(bf) for a in e]
    for h in heads:
        o_ref[:, cols[h]] = mm(p[h], v_ref[:, cols[h]], 1, 0).astype(bf)
        x_ref[h] = x[h][0]
        m_ref[h] = m[h][0]
        p_ref[h] = p[h]


def backward_kernel(
    first_ref, q_ref, k_ref, v_ref, path_ref, logit_ref, taps_ref, x_ref, m_ref, p_ref, do_ref,
    dqk_ref, dvp_ref, dlogit_ref, dtaps_ref,
):
    first = first_ref[0]
    rows = q_ref.shape[0]
    base = pl.program_id(0) * HB
    heads = range(HB)
    cols = [slice(h * DH, (h + 1) * DH) for h in heads]
    i, j = index((rows, rows))
    allowed = (i >= j) & ((i < first) | (j >= first))
    q = [q_ref[:, c] for c in cols]
    k = [k_ref[:, c] for c in cols]
    do = [do_ref[:, c].astype(bf) for c in cols]
    path = [path_ref[:, c] for c in cols]
    dirs = [directions(path[h], taps_ref[:, cols[h]], first) for h in heads]
    w = [d[0] for d in dirs]
    wb = [a.astype(bf) for a in w]
    logits = logit_ref[...]
    beta = [2.0 * jax.nn.sigmoid(column(logits, base + h)) for h in heads]
    p = [p_ref[h] for h in heads]
    x = [x_ref[h] for h in heads]
    m = [m_ref[h] for h in heads]
    dp = [mm(do[h], v_ref[:, cols[h]], 1, 1) for h in heads]
    for h in heads:
        dvp_ref[0, :, cols[h]] = mm(p[h], do[h], 0, 0).astype(bf)
    p = [a.astype(f32) for a in p]
    sums = [jnp.sum(dp[h] * p[h], axis=1, keepdims=True) for h in heads]
    ds = [jnp.where(allowed, p[h] * (dp[h] - sums[h]) * DH**-0.5, 0.0).astype(bf) for h in heads]
    wk = [jnp.where(i > j, mm(wb[h], k[h], 1, 1), 0.0) for h in heads]
    gram = [mm(wb[h], wb[h], 1, 1) for h in heads]
    dm = [(-mm(ds[h], (beta[h] * wk[h]).astype(bf), 1, 1)).astype(bf) for h in heads]
    dwk = [jnp.where(i > j, -mm(m[h], ds[h], 0, 0), 0.0) for h in heads]
    z = [mm(dm[h], x[h], 1, 1) for h in heads]
    dbeta = [jnp.sum(dwk[h] * wk[h], axis=1, keepdims=True) for h in heads]
    dwk = [(beta[h] * dwk[h]).astype(bf) for h in heads]
    da = [jnp.where(i > j, -mm(m[h], z[h].astype(bf), 0, 0), 0.0) for h in heads]
    dqw = [jnp.where(i >= j, z[h], 0.0).astype(bf) for h in heads]
    dbeta = [dbeta[h] + jnp.sum(da[h] * gram[h], axis=1, keepdims=True) for h in heads]
    dg = [(beta[h] * da[h]).astype(bf) for h in heads]
    dw = [mm(dg[h], wb[h], 1, 0) + mm(dg[h], wb[h], 0, 0) + mm(dqw[h], q[h], 0, 0) + mm(dwk[h], k[h], 1, 0) for h in heads]
    for h in heads:
        dqk_ref[0, :, cols[h]] = (mm(ds[h], k[h], 1, 0) + mm(dqw[h], wb[h], 1, 0)).astype(bf)
        dqk_ref[1, :, cols[h]] = (mm(ds[h], q[h], 0, 0) + mm(dwk[h], wb[h], 0, 0)).astype(bf)
    lane = lax.broadcasted_iota(jnp.int32, logits.shape, 1)
    out = jnp.zeros_like(logits)
    for h in heads:
        out = out + jnp.where(lane == base + h, dbeta[h] * (beta[h] * (1.0 - 0.5 * beta[h])), 0.0)
        r = dirs[h][1]
        dc = r * (dw[h] - w[h] * jnp.sum(w[h] * dw[h], axis=1, keepdims=True))
        taps = taps_ref[:, cols[h]]
        dpath = dc * taps[0:1]
        dtaps = [jnp.sum(dc * path[h], axis=0, keepdims=True)]
        for s in range(1, taps.shape[0]):
            up = shift_up(jnp.where(kept(dc.shape, s, first), dc, 0.0), s)
            dpath = dpath + up * taps[s : s + 1]
            dtaps.append(jnp.sum(up * path[h], axis=0, keepdims=True))
        dvp_ref[1, :, cols[h]] = dpath.astype(bf)
        dtaps_ref[:, cols[h]] = jnp.concatenate(dtaps, axis=0)

    @pl.when(pl.program_id(0) == 0)
    def _():
        dlogit_ref[...] = out

    @pl.when(pl.program_id(0) > 0)
    def _():
        dlogit_ref[...] += out


VM = 60 * 1024 * 1024


def specs(rows, ntaps, nh):
    wide = pl.BlockSpec((rows, HB * DH), lambda n: (0, n))
    square = pl.BlockSpec((HB, rows, rows), lambda n: (n, 0, 0))
    logit = pl.BlockSpec((rows, nh), lambda n: (0, 0))
    taps = pl.BlockSpec((ntaps, HB * DH), lambda n: (0, n))
    smem = pl.BlockSpec(memory_space=pltpu.SMEM)
    return wide, square, logit, taps, smem


def mix_forward(first, q, k, v, path, logit, taps):
    rows, width = q.shape
    nh = width // DH
    wide, square, lg, tp, sm = specs(rows, taps.shape[0], nh)
    sq = jax.ShapeDtypeStruct((nh, rows, rows), bf)
    return pl.pallas_call(
        forward_kernel,
        grid=(nh // HB,),
        in_specs=[sm, wide, wide, wide, wide, lg, tp],
        out_specs=[wide, square, square, square],
        out_shape=[jax.ShapeDtypeStruct((rows, width), bf), sq, sq, sq],
        compiler_params=pltpu.CompilerParams(vmem_limit_bytes=VM),
        cost_estimate=pl.CostEstimate(flops=12000000000, bytes_accessed=6000000, transcendentals=0),
        name="mix_forward",
    )(first, q, k, v, path, logit, taps)


def mix_backward(first, q, k, v, path, logit, taps, x, m, p, do):
    rows, width = q.shape
    nh = width // DH
    wide, square, lg, tp, sm = specs(rows, taps.shape[0], nh)
    low = jax.ShapeDtypeStruct((2, rows, width), bf)
    pair = pl.BlockSpec((2, rows, HB * DH), lambda n: (0, 0, n))
    return pl.pallas_call(
        backward_kernel,
        grid=(nh // HB,),
        in_specs=[sm, wide, wide, wide, wide, lg, tp, square, square, square, wide],
        out_specs=[pair, pair, lg, tp],
        out_shape=[low, low, jax.ShapeDtypeStruct((rows, nh), f32), jax.ShapeDtypeStruct(taps.shape, f32)],
        compiler_params=pltpu.CompilerParams(vmem_limit_bytes=VM),
        cost_estimate=pl.CostEstimate(flops=9000000000, bytes_accessed=6000000, transcendentals=0),
        name="mix_backward",
    )(first, q, k, v, path, logit, taps, x, m, p, do)


def dot_trans(left, right):
    return lax.dot_general(left, right, (((1,), (1,)), ((), ())), preferred_element_type=f32)


def dot(left, right):
    return jnp.dot(left, right, preferred_element_type=f32)


def product_kernel(near, far, b0, b1, away_ref, keep_ref):
    total = (mm(near[...], b0[0], 1, 0) + mm(far[...], b1[0], 1, 0)).astype(bf)
    half = total.shape[0] // 2
    away_ref[...] = total[:half]
    keep_ref[...] = total[half:]


def product(left, rights):
    near, far = left
    rows, slots = near.shape
    rights = [right.reshape((-1, slots, right.shape[-1])) for right in rights]
    count, _, width = rights[0].shape
    tile = 512 if width % 512 == 0 else 384
    tiles = width // tile
    half = jax.ShapeDtypeStruct((rows // 2, count * width), bf)
    return pl.pallas_call(
        product_kernel,
        grid=(count, tiles),
        in_specs=[pl.BlockSpec((rows, slots), lambda c, n: (0, 0))] * 2
        + [pl.BlockSpec((1, slots, tile), lambda c, n: (c, 0, n))] * 2,
        out_specs=[pl.BlockSpec((rows // 2, tile), lambda c, n: (0, c * tiles + n))] * 2,
        out_shape=[half, half],
        compiler_params=pltpu.CompilerParams(vmem_limit_bytes=VM // 2),
        cost_estimate=pl.CostEstimate(
            flops=4 * 10**6 * width * count // 3, bytes_accessed=2000 * width * count, transcendentals=0
        ),
        name="product",
    )(near, far, *rights)


def turn_kernel(blocks_ref, own_ref, near_ref, far_ref, turned):
    count = near_ref.shape[0] // blocks_ref.shape[1]
    for n in range(own_ref.shape[1] // DH):
        turned[n * DH : (n + 1) * DH, :] = own_ref[:, n * DH : (n + 1) * DH].T
    for which, out in enumerate((near_ref, far_ref)):
        for n in range(blocks_ref.shape[1]):
            start = pl.multiple_of(blocks_ref[which, n] * count, 16)
            out[n * count : (n + 1) * count, :] = turned[pl.ds(start, count), :]


def turn(blocks, own):
    slots, features = own.shape
    rows = features // 2
    out = jax.ShapeDtypeStruct((rows, slots), bf)
    per = rows // blocks.shape[1]
    if per % 16:
        turned = own.T.reshape(features // per, per, slots)
        return [turned[blocks[n]].reshape(rows, slots) for n in range(2)]
    vmem = pl.BlockSpec(memory_space=pltpu.VMEM)
    return pl.pallas_call(
        turn_kernel,
        in_specs=[pl.BlockSpec(memory_space=pltpu.SMEM), vmem],
        out_specs=[vmem, vmem],
        out_shape=[out, out],
        scratch_shapes=[pltpu.VMEM((features, slots), bf)],
        compiler_params=pltpu.CompilerParams(vmem_limit_bytes=VM // 2),
        cost_estimate=pl.CostEstimate(flops=0, bytes_accessed=4 * slots * features, transcendentals=0),
        name="turn",
    )(blocks, own)


def back_kernel(first, second, w0, w1, w2, w3, o_ref):
    total = mm(first[0], w0[...], 1, 1) + mm(first[1], w1[...], 1, 1)
    o_ref[...] = total + mm(second[0], w2[...], 1, 1) + mm(second[1], w3[...], 1, 1)


def back(first, second, weights):
    _, slots, width = first.shape
    depth = weights[0].shape[0]
    tile = 512 if depth % 512 == 0 else DH
    return pl.pallas_call(
        back_kernel,
        grid=(depth // tile,),
        in_specs=[pl.BlockSpec((2, slots, width), lambda n: (0, 0, 0))] * 2
        + [pl.BlockSpec((tile, width), lambda n: (n, 0))] * 4,
        out_specs=pl.BlockSpec((slots, tile), lambda n: (0, n)),
        out_shape=jax.ShapeDtypeStruct((slots, depth), f32),
        compiler_params=pltpu.CompilerParams(vmem_limit_bytes=VM // 2),
        cost_estimate=pl.CostEstimate(flops=5 * 10**9, bytes_accessed=11 * 10**6, transcendentals=0),
        name="back",
    )(first, second, *weights)


def after(array, *others):
    return lax.optimization_barrier((array,) + others)[0]


def pick(array, which, axis=0):
    return lax.dynamic_index_in_dim(array, which, axis, keepdims=False)


class Links:
    def __init__(self):
        self.count = lax.axis_size("dp")
        self.pair_last = ()
        self.line = self.count // 4
        self.me = lax.axis_index("dp")
        self.core = self.me % 2
        self.pair = (self.me // 2) % 2
        self.place = self.me // 4
        places = [self.place]
        bit = self.line // 2
        while bit >= 1:
            places = [p ^ bit for p in places] + places
            bit //= 2

        def listed(places):
            chips = [
                jnp.concatenate([4 * places + 2 * pair + 1 - self.core, 4 * places + 2 * pair + self.core])
                for pair in (self.pair, 1 - self.pair)
            ]
            return jnp.stack(chips).astype(jnp.int32)

        self.halving = listed(jnp.stack(places))
        self.in_line = listed(jnp.arange(self.line, dtype=jnp.int32))
        self.lines = [[4 * place + n for place in range(self.line)] for n in range(4)]

    def flip(self, array, bit):
        return lax.ppermute(array, "dp", [(i, i ^ bit) for i in range(self.count)])

    def left(self, array, blocks):
        near, away = turn(blocks, array)
        return near, self.pair_rows(away)

    def pair_rows(self, array, together=1):
        got = self.flip(after(array, *self.pair_last[: 3 - together]), 2)
        self.pair_last = self.pair_last[-1:] + (got,)
        return got

    def chosen(self, array):
        own = self.halving[0, self.line :]
        return jnp.concatenate([pick(array, own[n]) for n in range(self.line)], axis=0)

    def cores(self, halves):
        away, keep = halves
        return keep + self.flip(away, 1)

    def scatter(self, partial):
        return lax.psum_scatter(
            partial, "dp", scatter_dimension=0, axis_index_groups=self.lines, tiled=True
        ).astype(f32)

    def first(self, total):
        half = total.shape[0] // 2
        away, keep = total[:half], total[half:]
        bit = 1
        while 2 * bit <= self.line // 2:
            got = self.flip(away, 4 * bit)
            half = keep.shape[0] // 2
            away, keep = keep[:half] + got[:half], keep[half:] + got[half:]
            bit *= 2
        return away, keep

    def second(self, halves, *before):
        away, keep = halves
        got = self.flip(away, 2 * self.line)
        return keep.astype(f32) + after(got, *before).astype(f32)


def swap(array):
    return lax.ppermute(array, "head", [(0, 1), (1, 0)])


def in_order(own, other, place):
    return jnp.concatenate([jnp.where(place == 0, own, other), jnp.where(place == 0, other, own)], axis=0)


def norm_back(grad, values, gain, scale):
    scaled = gain * grad
    mean = jnp.mean(scaled * values, axis=1, keepdims=True)
    return scale * scaled - values * (scale * scale * scale) * mean


def norm_scale(values):
    return lax.rsqrt(jnp.mean(values * values, axis=1, keepdims=True) + 1e-6)


def per_device(
    tokens,
    norm1_gain,
    w_query,
    w_key,
    w_value,
    w_path,
    w_beta,
    conv_kernel,
    w_output,
    norm2_gain,
    w_gate,
    w_up,
    w_down,
    item_lengths,
    cotangent,
):
    links = Links()
    head = lax.axis_index("head")
    local = tokens.shape[0]
    depth = tokens.shape[1]

    tokens_other = swap(tokens)
    tokens_all = in_order(tokens, tokens_other, head)

    quarter = 2 * links.pair + links.core
    quarters = w_output.reshape(4, depth // 4, w_output.shape[1])
    got = swap(after(pick(quarters, quarter), tokens_other))
    cot_other = swap(after(cotangent, got))
    cot_all = in_order(cotangent, cot_other, head)

    inputs = tokens_all.astype(f32)
    scale1 = norm_scale(inputs)
    normed1 = (inputs * scale1 * norm1_gain).astype(bf)
    queries = dot(normed1, w_query).astype(bf)
    keys = dot(normed1, w_key).astype(bf)
    values = dot(normed1, w_value).astype(bf)
    path_raw = dot(normed1, w_path)
    beta_logit = dot(normed1, w_beta)
    taps = jnp.transpose(conv_kernel, (2, 1, 0)).reshape(conv_kernel.shape[2], -1)

    queries = after(queries, got)
    got_pair = links.pair_rows(got)
    mixed, solved, moved, probs = mix_forward(item_lengths, queries, keys, values, path_raw, beta_logit, taps)
    mixed_other = swap(after(mixed, cot_other, got_pair))
    got_core = links.flip(jnp.stack([got, after(got_pair, mixed)]), 1)
    left_cot = links.left(after(cot_all, mixed), links.in_line)

    def chosen(pair, core):
        near = jnp.where(core == links.core, got, got_core[0])
        far = jnp.where(core == links.core, got_pair, got_core[1])
        return jnp.where(pair == links.pair, near, far)

    w_output_other = jnp.concatenate([chosen(0, 0), chosen(0, 1), chosen(1, 0), chosen(1, 1)], axis=0)
    near_one, far_one = turn(links.halving, normed1)
    mixed_other = after(mixed_other, near_one)
    resid = inputs + dot_trans(mixed, w_output) + dot_trans(mixed_other, w_output_other)
    scale2 = norm_scale(resid)
    normed2 = (resid * scale2 * norm2_gain).astype(bf)
    near_two, far_two = turn(links.in_line, normed2)
    gate = dot(normed2, w_gate)
    upper = dot(normed2, w_up)
    sigma = jax.nn.sigmoid(gate)
    activated = gate * sigma
    gate, upper, hidden = lax.optimization_barrier((gate, upper, (activated * upper).astype(bf)))
    sigma = jax.nn.sigmoid(gate)
    activated = gate * sigma
    grad_hidden = dot(cot_all, w_down)
    grad_gate = (grad_hidden * upper * (sigma * (1.0 + gate * (1.0 - sigma)))).astype(bf)
    grad_upper = (grad_hidden * activated).astype(bf)

    pairs_hidden = links.pair_rows(after(hidden, near_two))
    part2 = dot_trans(grad_gate, w_gate) + dot_trans(grad_upper, w_up)
    other2 = swap(part2.astype(bf))
    total_down = links.cores(product(left_cot, (after(hidden, other2), pairs_hidden)))
    grad_w_down = links.scatter(total_down)
    pairs_gate = links.pair_rows(grad_gate)

    other2 = after(other2, total_down)
    grad_normed2 = part2 + other2.astype(f32)
    grad_gain2 = jnp.sum(grad_normed2 * resid * scale2, axis=0, keepdims=True)
    grad_resid = cot_all.astype(f32) + norm_back(grad_normed2, resid, norm2_gain, scale2)
    branch = grad_resid.astype(bf)
    grad_mixed = dot(branch, w_output).astype(bf)
    grad_qk, grad_vp, grad_logit, grad_taps = mix_backward(
        item_lengths, queries, keys, values, path_raw, beta_logit, taps, solved, moved, probs, grad_mixed
    )

    def halves(array):
        return array.reshape(2, local, depth)

    left_two = near_two, links.pair_rows(after(far_two, grad_qk))
    pairs_up = links.pair_rows(grad_upper)
    near_branch, far_branch = turn(links.halving, after(branch, grad_qk))
    left_one = near_one, links.pair_rows(far_one)
    product_gate = product(left_two, (after(grad_gate, grad_qk), pairs_gate))
    total_gate = links.cores(product_gate)
    grad_w_gate = links.scatter(total_gate)
    low_logit = grad_logit.astype(bf)
    part = back(after(grad_qk, total_gate, near_branch, grad_w_down), grad_vp, (w_query, w_key, w_value, w_path))
    part = halves(part + dot_trans(low_logit, w_beta))
    part_away = pick(part, 1 - head).astype(bf)
    other1 = swap(part_away)
    part_keep = pick(part, head)
    total_up = links.cores(product(left_two, (after(grad_upper, part_away), pairs_up)))
    grad_w_up = links.scatter(total_up)
    pairs_qk = links.pair_rows(grad_qk)
    other1 = after(other1, total_up)
    grad_normed1 = part_keep + other1.astype(f32)
    inputs_own = tokens.astype(f32)
    scale_own = norm_scale(inputs_own)
    grad_tokens = pick(halves(grad_resid), head) + norm_back(grad_normed1, inputs_own, norm1_gain, scale_own)
    grad_gain1 = jnp.sum(grad_normed1 * inputs_own * scale_own, axis=0, keepdims=True)

    width = w_query.shape[1]
    low_logit, grad_gain2 = after(low_logit, total_up), after(grad_gain2, total_up)
    grad_taps = after(grad_taps, total_up)
    small = lax.dot_general(low_logit, normed1, (((0,), (0,)), ((), ())), preferred_element_type=f32)
    grad_gain1 = grad_gain1 + swap(grad_gain1)
    small = jnp.concatenate([small, grad_gain1, grad_gain2], axis=0)
    heads = w_beta.shape[1]
    rows = depth // links.count
    conv_rows = conv_kernel.shape[0] // links.count
    small = jnp.swapaxes(small.reshape(-1, links.count, rows), 0, 1)
    conv = jnp.swapaxes(grad_taps.reshape(-1, links.count, conv_rows), 0, 1).reshape(links.count, 2, rows)
    small = jnp.concatenate([small, conv], axis=1)
    small = jnp.pad(small, ((0, 0), (0, 16 - small.shape[1]), (0, DH - rows)))

    left_branch = near_branch, links.pair_rows(after(far_branch, total_up, small))
    pairs_vp = links.pair_rows(grad_vp)
    pairs_mixed = links.pair_rows(mixed, 2)
    total_qk = links.cores(product(left_one, (after(grad_qk, grad_w_gate, small), pairs_qk)))
    first_qk = links.first(total_qk)
    total_vp = links.cores(product(left_one, (after(grad_vp, grad_w_up, first_qk[0]), pairs_vp)))
    first_vp = links.first(total_vp)
    hidden_late = after(hidden, total_vp)
    part = halves(dot_trans(hidden_late, w_down))
    ffn_away = pick(part, 1 - head).astype(bf)
    ffn = swap(after(ffn_away, other1))
    resid_own = pick(halves(resid), head)
    activations = (resid_own + pick(part, head) + ffn.astype(f32)).astype(bf)
    sum_qk = links.second(first_qk)
    total_output = links.cores(product(left_branch, (after(mixed, total_vp), pairs_mixed)))
    first_output = links.first(total_output)
    sum_vp = links.second(first_vp)
    grad_w_output = links.second(first_output)
    core_small = small + links.flip(small, 1)
    pair_small = core_small + links.pair_rows(after(core_small, first_vp[0]))
    small = links.second(links.first(links.chosen(pair_small)))[:, :rows]

    width = w_query.shape[1]
    grad_w_beta = small[:heads].T
    piece = rows // 2
    gains = lax.dynamic_slice_in_dim(small[heads : heads + 2], piece * head, piece, 1)
    conv = small[heads + 2 : heads + 4].reshape(-1, heads, conv_rows)
    grad_conv = jnp.transpose(conv, (2, 1, 0))

    grad_gain1, grad_gain2 = gains[0], gains[1]
    grad_w_query, grad_w_key = sum_qk[:, :width], sum_qk[:, width:]
    grad_w_value, grad_w_path = sum_vp[:, :width], sum_vp[:, width:]
    return (
        activations,
        grad_tokens,
        grad_gain1,
        grad_w_query,
        grad_w_key,
        grad_w_value,
        grad_w_path,
        grad_w_beta,
        grad_conv,
        grad_w_output,
        grad_gain2,
        grad_w_gate,
        grad_w_up,
        grad_w_down,
    )


def solution(mesh):
    in_specs = (
        P(("dp", "head"), None),
        P(),
        P(None, "head"),
        P(None, "head"),
        P(None, "head"),
        P(None, "head"),
        P(None, "head"),
        P(None, "head", None),
        P(None, "head"),
        P(),
        P(None, "head"),
        P(None, "head"),
        P(None, "head"),
        P("dp"),
        P(("dp", "head"), None),
    )
    out_specs = (
        P(("dp", "head"), None),
        P(("dp", "head"), None),
        P(("dp", "head")),
        P("dp", "head"),
        P("dp", "head"),
        P("dp", "head"),
        P("dp", "head"),
        P("dp", "head"),
        P("dp", "head", None),
        P("dp", "head"),
        P(("dp", "head")),
        P("dp", "head"),
        P("dp", "head"),
        P("dp", "head"),
    )
    return jax.shard_map(
        per_device, mesh=mesh, in_specs=in_specs, out_specs=out_specs, check_vma=False
    )
```

```python
import jax
import jax.numpy as jnp
from jax import lax
from jax.experimental import pallas as pl
from jax.experimental.pallas import tpu as pltpu
from jax.sharding import PartitionSpec as P

f32 = jnp.float32
bf = jnp.bfloat16
DH = 128
HB = 3


def mm(a, b, ca, cb):
    return lax.dot_general(a, b, (((ca,), (cb,)), ((), ())), preferred_element_type=f32)


def parts(a):
    high = a.astype(bf)
    return high, (a - high.astype(f32)).astype(bf)


def mm3(a, b, ca, cb):
    (ah, al), (bh, bl) = a, b
    return mm(ah, bh, ca, cb) + mm(ah, bl, ca, cb) + mm(al, bh, ca, cb)


def mm2(a, b, ca, cb):
    return mm(a, b[0], ca, cb) + mm(a, b[1], ca, cb)


def index(shape):
    return lax.broadcasted_iota(jnp.int32, shape, 0), lax.broadcasted_iota(jnp.int32, shape, 1)


def column(array, which):
    lane = lax.broadcasted_iota(jnp.int32, array.shape, 1)
    return jnp.sum(jnp.where(lane == which, array, 0.0), axis=1, keepdims=True)


def shift_down(a, s):
    return jnp.concatenate([jnp.zeros((s, a.shape[1]), a.dtype), a[: a.shape[0] - s]], axis=0)


def shift_up(a, s):
    return jnp.concatenate([a[s:], jnp.zeros((s, a.shape[1]), a.dtype)], axis=0)


def kept(shape, s, first):
    t = lax.broadcasted_iota(jnp.int32, shape, 0)
    return (t >= s) & ~((t >= first) & (t - s < first))


def directions(path, taps, first):
    total = path * taps[0:1]
    for s in range(1, taps.shape[0]):
        total = total + jnp.where(kept(path.shape, s, first), shift_down(path, s), 0.0) * taps[s : s + 1]
    r = lax.rsqrt(jnp.sum(total * total, axis=1, keepdims=True) + 1e-6)
    return total * r, r


def inverses(systems):
    size = systems[0].shape[0]
    i, j = index((size, size))
    solved = [jnp.where(i == j, 1.0, 0.0) - jnp.where(i // 2 == j // 2, a, 0.0) for a in systems]
    width = 2
    while width < size:
        inside = (i // (2 * width) == j // (2 * width)) & (i // width != j // width)
        offs = [parts(jnp.where(inside, a, 0.0)) for a in systems]
        lows = [parts(x) for x in solved]
        inner = [parts(mm3(o, x, 1, 0)) for o, x in zip(offs, lows)]
        solved = [x - mm3(l, y, 1, 0) for x, l, y in zip(solved, lows, inner)]
        width *= 2
    return solved


def forward_kernel(first_ref, q_ref, k_ref, v_ref, path_ref, logit_ref, taps_ref, o_ref, x_ref, m_ref, p_ref):
    first = first_ref[0]
    rows = q_ref.shape[0]
    half = rows // 2
    base = pl.program_id(0) * HB
    heads = range(HB)
    cols = [slice(h * DH, (h + 1) * DH) for h in heads]
    i, j = index((rows, rows))
    q = [q_ref[:, c] for c in cols]
    k = [k_ref[:, c] for c in cols]
    w = [parts(directions(path_ref[:, c], taps_ref[:, c], first)[0]) for c in cols]
    logits = logit_ref[...]
    beta = [2.0 * jax.nn.sigmoid(column(logits, base + h)) for h in heads]
    system = [jnp.where(i > j, beta[h] * mm3(w[h], w[h], 1, 1), 0.0) for h in heads]
    corners = inverses([s[:half, :half] for s in system] + [s[half:, half:] for s in system])
    corners = [parts(x) for x in corners]
    low = [parts(mm3(parts(system[h][half:, :half]), corners[h], 1, 0)) for h in heads]
    low = [parts(-mm3(corners[HB + h], low[h], 1, 0)) for h in heads]
    zero = jnp.zeros((half, half), bf)
    x = [
        tuple(
            jnp.concatenate(
                [
                    jnp.concatenate([corners[h][n], zero], axis=1),
                    jnp.concatenate([low[h][n], corners[HB + h][n]], axis=1),
                ],
                axis=0,
            )
            for n in range(2)
        )
        for h in heads
    ]
    qw = [parts(jnp.where(i >= j, mm2(q[h], w[h], 1, 1), 0.0)) for h in heads]
    wk = [mm(w[h][0], k[h], 1, 1) + mm(w[h][1], k[h], 1, 1) for h in heads]
    wk = [parts(jnp.where(i > j, beta[h] * wk[h], 0.0)) for h in heads]
    m = [parts(mm3(qw[h], x[h], 1, 0)) for h in heads]
    s = [mm(q[h], k[h], 1, 1) - mm3(m[h], wk[h], 1, 0) for h in heads]
    allowed = (i >= j) & ((i < first) | (j >= first))
    s = [jnp.where(allowed, a * DH**-0.5, -1e30) for a in s]
    e = [jnp.exp(a - jnp.max(a, axis=1, keepdims=True)) for a in s]
    p = [(a / jnp.sum(a, axis=1, keepdims=True)).astype(bf) for a in e]
    for h in heads:
        o_ref[:, cols[h]] = mm(p[h], v_ref[:, cols[h]], 1, 0).astype(bf)
        x_ref[h] = x[h][0]
        m_ref[h] = m[h][0]
        p_ref[h] = p[h]


def backward_kernel(
    first_ref, q_ref, k_ref, v_ref, path_ref, logit_ref, taps_ref, x_ref, m_ref, p_ref, do_ref,
    dqk_ref, dvp_ref, dlogit_ref, dtaps_ref,
):
    first = first_ref[0]
    rows = q_ref.shape[0]
    base = pl.program_id(0) * HB
    heads = range(HB)
    cols = [slice(h * DH, (h + 1) * DH) for h in heads]
    i, j = index((rows, rows))
    allowed = (i >= j) & ((i < first) | (j >= first))
    q = [q_ref[:, c] for c in cols]
    k = [k_ref[:, c] for c in cols]
    do = [do_ref[:, c].astype(bf) for c in cols]
    path = [path_ref[:, c] for c in cols]
    dirs = [directions(path[h], taps_ref[:, cols[h]], first) for h in heads]
    w = [d[0] for d in dirs]
    wb = [a.astype(bf) for a in w]
    logits = logit_ref[...]
    beta = [2.0 * jax.nn.sigmoid(column(logits, base + h)) for h in heads]
    p = [p_ref[h] for h in heads]
    x = [x_ref[h] for h in heads]
    m = [m_ref[h] for h in heads]
    dp = [mm(do[h], v_ref[:, cols[h]], 1, 1) for h in heads]
    for h in heads:
        dvp_ref[0, :, cols[h]] = mm(p[h], do[h], 0, 0).astype(bf)
    p = [a.astype(f32) for a in p]
    sums = [jnp.sum(dp[h] * p[h], axis=1, keepdims=True) for h in heads]
    ds = [jnp.where(allowed, p[h] * (dp[h] - sums[h]) * DH**-0.5, 0.0).astype(bf) for h in heads]
    wk = [jnp.where(i > j, mm(wb[h], k[h], 1, 1), 0.0) for h in heads]
    gram = [mm(wb[h], wb[h], 1, 1) for h in heads]
    dm = [(-mm(ds[h], (beta[h] * wk[h]).astype(bf), 1, 1)).astype(bf) for h in heads]
    dwk = [jnp.where(i > j, -mm(m[h], ds[h], 0, 0), 0.0) for h in heads]
    z = [mm(dm[h], x[h], 1, 1) for h in heads]
    dbeta = [jnp.sum(dwk[h] * wk[h], axis=1, keepdims=True) for h in heads]
    dwk = [(beta[h] * dwk[h]).astype(bf) for h in heads]
    da = [jnp.where(i > j, -mm(m[h], z[h].astype(bf), 0, 0), 0.0) for h in heads]
    dqw = [jnp.where(i >= j, z[h], 0.0).astype(bf) for h in heads]
    dbeta = [dbeta[h] + jnp.sum(da[h] * gram[h], axis=1, keepdims=True) for h in heads]
    dg = [(beta[h] * da[h]).astype(bf) for h in heads]
    dw = [mm(dg[h], wb[h], 1, 0) + mm(dg[h], wb[h], 0, 0) + mm(dqw[h], q[h], 0, 0) + mm(dwk[h], k[h], 1, 0) for h in heads]
    for h in heads:
        dqk_ref[0, :, cols[h]] = (mm(ds[h], k[h], 1, 0) + mm(dqw[h], wb[h], 1, 0)).astype(bf)
        dqk_ref[1, :, cols[h]] = (mm(ds[h], q[h], 0, 0) + mm(dwk[h], wb[h], 0, 0)).astype(bf)
    lane = lax.broadcasted_iota(jnp.int32, logits.shape, 1)
    out = jnp.zeros_like(logits)
    for h in heads:
        out = out + jnp.where(lane == base + h, dbeta[h] * (beta[h] * (1.0 - 0.5 * beta[h])), 0.0)
        r = dirs[h][1]
        dc = r * (dw[h] - w[h] * jnp.sum(w[h] * dw[h], axis=1, keepdims=True))
        taps = taps_ref[:, cols[h]]
        dpath = dc * taps[0:1]
        dtaps = [jnp.sum(dc * path[h], axis=0, keepdims=True)]
        for s in range(1, taps.shape[0]):
            up = shift_up(jnp.where(kept(dc.shape, s, first), dc, 0.0), s)
            dpath = dpath + up * taps[s : s + 1]
            dtaps.append(jnp.sum(up * path[h], axis=0, keepdims=True))
        dvp_ref[1, :, cols[h]] = dpath.astype(bf)
        dtaps_ref[:, cols[h]] = jnp.concatenate(dtaps, axis=0)

    @pl.when(pl.program_id(0) == 0)
    def _():
        dlogit_ref[...] = out

    @pl.when(pl.program_id(0) > 0)
    def _():
        dlogit_ref[...] += out


VM = 60 * 1024 * 1024


def specs(rows, ntaps, nh):
    wide = pl.BlockSpec((rows, HB * DH), lambda n: (0, n))
    square = pl.BlockSpec((HB, rows, rows), lambda n: (n, 0, 0))
    logit = pl.BlockSpec((rows, nh), lambda n: (0, 0))
    taps = pl.BlockSpec((ntaps, HB * DH), lambda n: (0, n))
    smem = pl.BlockSpec(memory_space=pltpu.SMEM)
    return wide, square, logit, taps, smem


def mix_forward(first, q, k, v, path, logit, taps):
    rows, width = q.shape
    nh = width // DH
    wide, square, lg, tp, sm = specs(rows, taps.shape[0], nh)
    sq = jax.ShapeDtypeStruct((nh, rows, rows), bf)
    return pl.pallas_call(
        forward_kernel,
        grid=(nh // HB,),
        in_specs=[sm, wide, wide, wide, wide, lg, tp],
        out_specs=[wide, square, square, square],
        out_shape=[jax.ShapeDtypeStruct((rows, width), bf), sq, sq, sq],
        compiler_params=pltpu.CompilerParams(vmem_limit_bytes=VM),
        cost_estimate=pl.CostEstimate(flops=12000000000, bytes_accessed=6000000, transcendentals=0),
        name="mix_forward",
    )(first, q, k, v, path, logit, taps)


def mix_backward(first, q, k, v, path, logit, taps, x, m, p, do):
    rows, width = q.shape
    nh = width // DH
    wide, square, lg, tp, sm = specs(rows, taps.shape[0], nh)
    low = jax.ShapeDtypeStruct((2, rows, width), bf)
    pair = pl.BlockSpec((2, rows, HB * DH), lambda n: (0, 0, n))
    return pl.pallas_call(
        backward_kernel,
        grid=(nh // HB,),
        in_specs=[sm, wide, wide, wide, wide, lg, tp, square, square, square, wide],
        out_specs=[pair, pair, lg, tp],
        out_shape=[low, low, jax.ShapeDtypeStruct((rows, nh), f32), jax.ShapeDtypeStruct(taps.shape, f32)],
        compiler_params=pltpu.CompilerParams(vmem_limit_bytes=VM),
        cost_estimate=pl.CostEstimate(flops=9000000000, bytes_accessed=6000000, transcendentals=0),
        name="mix_backward",
    )(first, q, k, v, path, logit, taps, x, m, p, do)


def dot_trans(left, right):
    return lax.dot_general(left, right, (((1,), (1,)), ((), ())), preferred_element_type=f32)


def dot(left, right):
    return jnp.dot(left, right, preferred_element_type=f32)


def product_kernel(near, far, b0, b1, away_ref, keep_ref):
    total = (mm(near[...], b0[0], 1, 0) + mm(far[...], b1[0], 1, 0)).astype(bf)
    half = total.shape[0] // 2
    away_ref[...] = total[:half]
    keep_ref[...] = total[half:]


def product(left, rights):
    near, far = left
    rows, slots = near.shape
    rights = [right.reshape((-1, slots, right.shape[-1])) for right in rights]
    count, _, width = rights[0].shape
    tile = 1024 if width % 1024 == 0 else width
    tiles = width // tile
    half = jax.ShapeDtypeStruct((rows // 2, count * width), bf)
    return pl.pallas_call(
        product_kernel,
        grid=(count, tiles),
        in_specs=[pl.BlockSpec((rows, slots), lambda c, n: (0, 0))] * 2
        + [pl.BlockSpec((1, slots, tile), lambda c, n: (c, 0, n))] * 2,
        out_specs=[pl.BlockSpec((rows // 2, tile), lambda c, n: (0, c * tiles + n))] * 2,
        out_shape=[half, half],
        compiler_params=pltpu.CompilerParams(vmem_limit_bytes=VM // 2),
        cost_estimate=pl.CostEstimate(
            flops=4 * 10**6 * width * count // 3, bytes_accessed=2000 * width * count, transcendentals=0
        ),
        name="product",
    )(near, far, *rights)


def turn_kernel(blocks_ref, own_ref, near_ref, far_ref, turned):
    count = near_ref.shape[0] // blocks_ref.shape[1]
    for n in range(own_ref.shape[1] // DH):
        turned[n * DH : (n + 1) * DH, :] = own_ref[:, n * DH : (n + 1) * DH].T
    for which, out in enumerate((near_ref, far_ref)):
        for n in range(blocks_ref.shape[1]):
            start = pl.multiple_of(blocks_ref[which, n] * count, 16)
            out[n * count : (n + 1) * count, :] = turned[pl.ds(start, count), :]


def turn(blocks, own):
    slots, features = own.shape
    rows = features // 2
    out = jax.ShapeDtypeStruct((rows, slots), bf)
    per = rows // blocks.shape[1]
    if per % 16:
        turned = own.T.reshape(features // per, per, slots)
        return [turned[blocks[n]].reshape(rows, slots) for n in range(2)]
    vmem = pl.BlockSpec(memory_space=pltpu.VMEM)
    return pl.pallas_call(
        turn_kernel,
        in_specs=[pl.BlockSpec(memory_space=pltpu.SMEM), vmem],
        out_specs=[vmem, vmem],
        out_shape=[out, out],
        scratch_shapes=[pltpu.VMEM((features, slots), bf)],
        compiler_params=pltpu.CompilerParams(vmem_limit_bytes=VM // 2),
        cost_estimate=pl.CostEstimate(flops=0, bytes_accessed=4 * slots * features, transcendentals=0),
        name="turn",
    )(blocks, own)


def back_kernel(first, second, w0, w1, w2, w3, o_ref):
    total = mm(first[0], w0[...], 1, 1) + mm(first[1], w1[...], 1, 1)
    o_ref[...] = total + mm(second[0], w2[...], 1, 1) + mm(second[1], w3[...], 1, 1)


def back(first, second, weights):
    _, slots, width = first.shape
    depth = weights[0].shape[0]
    tile = 512 if depth % 512 == 0 else DH
    return pl.pallas_call(
        back_kernel,
        grid=(depth // tile,),
        in_specs=[pl.BlockSpec((2, slots, width), lambda n: (0, 0, 0))] * 2
        + [pl.BlockSpec((tile, width), lambda n: (n, 0))] * 4,
        out_specs=pl.BlockSpec((slots, tile), lambda n: (0, n)),
        out_shape=jax.ShapeDtypeStruct((slots, depth), f32),
        compiler_params=pltpu.CompilerParams(vmem_limit_bytes=VM // 2),
        cost_estimate=pl.CostEstimate(flops=5 * 10**9, bytes_accessed=11 * 10**6, transcendentals=0),
        name="back",
    )(first, second, *weights)


def after(array, *others):
    return lax.optimization_barrier((array,) + others)[0]


def pick(array, which, axis=0):
    return lax.dynamic_index_in_dim(array, which, axis, keepdims=False)


class Links:
    def __init__(self):
        self.count = lax.axis_size("dp")
        self.pair_last = ()
        self.line = self.count // 4
        self.me = lax.axis_index("dp")
        self.core = self.me % 2
        self.pair = (self.me // 2) % 2
        self.place = self.me // 4
        places = [self.place]
        bit = self.line // 2
        while bit >= 1:
            places = [p ^ bit for p in places] + places
            bit //= 2

        def listed(places):
            chips = [
                jnp.concatenate([4 * places + 2 * pair + 1 - self.core, 4 * places + 2 * pair + self.core])
                for pair in (self.pair, 1 - self.pair)
            ]
            return jnp.stack(chips).astype(jnp.int32)

        self.halving = listed(jnp.stack(places))
        self.in_line = listed(jnp.arange(self.line, dtype=jnp.int32))
        self.lines = [[4 * place + n for place in range(self.line)] for n in range(4)]

    def flip(self, array, bit):
        return lax.ppermute(array, "dp", [(i, i ^ bit) for i in range(self.count)])

    def left(self, array, blocks):
        near, away = turn(blocks, array)
        return near, self.pair_rows(away)

    def pair_rows(self, array, together=1):
        got = self.flip(after(array, *self.pair_last[: 3 - together]), 2)
        self.pair_last = self.pair_last[-1:] + (got,)
        return got

    def chosen(self, array):
        own = self.halving[0, self.line :]
        return jnp.concatenate([pick(array, own[n]) for n in range(self.line)], axis=0)

    def cores(self, halves):
        away, keep = halves
        return keep + self.flip(away, 1)

    def scatter(self, partial):
        return lax.psum_scatter(
            partial, "dp", scatter_dimension=0, axis_index_groups=self.lines, tiled=True
        ).astype(f32)

    def first(self, total):
        half = total.shape[0] // 2
        away, keep = total[:half], total[half:]
        bit = 1
        while 2 * bit <= self.line // 2:
            got = self.flip(away, 4 * bit)
            half = keep.shape[0] // 2
            away, keep = keep[:half] + got[:half], keep[half:] + got[half:]
            bit *= 2
        return away, keep

    def second(self, halves, *before):
        away, keep = halves
        got = self.flip(away, 2 * self.line)
        return keep.astype(f32) + after(got, *before).astype(f32)


def swap(array):
    return lax.ppermute(array, "head", [(0, 1), (1, 0)])


def in_order(own, other, place):
    return jnp.concatenate([jnp.where(place == 0, own, other), jnp.where(place == 0, other, own)], axis=0)


def norm_back(grad, values, gain, scale):
    scaled = gain * grad
    mean = jnp.mean(scaled * values, axis=1, keepdims=True)
    return scale * scaled - values * (scale * scale * scale) * mean


def norm_scale(values):
    return lax.rsqrt(jnp.mean(values * values, axis=1, keepdims=True) + 1e-6)


def per_device(
    tokens,
    norm1_gain,
    w_query,
    w_key,
    w_value,
    w_path,
    w_beta,
    conv_kernel,
    w_output,
    norm2_gain,
    w_gate,
    w_up,
    w_down,
    item_lengths,
    cotangent,
):
    links = Links()
    head = lax.axis_index("head")
    local = tokens.shape[0]
    depth = tokens.shape[1]

    tokens_other = swap(tokens)
    tokens_all = in_order(tokens, tokens_other, head)

    quarter = 2 * links.pair + links.core
    quarters = w_output.reshape(4, depth // 4, w_output.shape[1])
    got = swap(after(pick(quarters, quarter), tokens_other))
    cot_other = swap(after(cotangent, got))
    cot_all = in_order(cotangent, cot_other, head)

    inputs = tokens_all.astype(f32)
    scale1 = norm_scale(inputs)
    normed1 = (inputs * scale1 * norm1_gain).astype(bf)
    queries = dot(normed1, w_query).astype(bf)
    keys = dot(normed1, w_key).astype(bf)
    values = dot(normed1, w_value).astype(bf)
    path_raw = dot(normed1, w_path)
    beta_logit = dot(normed1, w_beta)
    taps = jnp.transpose(conv_kernel, (2, 1, 0)).reshape(conv_kernel.shape[2], -1)

    queries = after(queries, got)
    got_pair = links.pair_rows(got)
    mixed, solved, moved, probs = mix_forward(item_lengths, queries, keys, values, path_raw, beta_logit, taps)
    mixed_other = swap(after(mixed, cot_other, got_pair))
    got_core = links.flip(jnp.stack([got, after(got_pair, mixed)]), 1)
    left_cot = links.left(after(cot_all, mixed), links.in_line)

    def chosen(pair, core):
        near = jnp.where(core == links.core, got, got_core[0])
        far = jnp.where(core == links.core, got_pair, got_core[1])
        return jnp.where(pair == links.pair, near, far)

    w_output_other = jnp.concatenate([chosen(0, 0), chosen(0, 1), chosen(1, 0), chosen(1, 1)], axis=0)
    near_one, far_one = turn(links.halving, normed1)
    mixed_other = after(mixed_other, near_one)
    resid = inputs + dot_trans(mixed, w_output) + dot_trans(mixed_other, w_output_other)
    scale2 = norm_scale(resid)
    normed2 = (resid * scale2 * norm2_gain).astype(bf)
    near_two, far_two = turn(links.in_line, normed2)
    gate = dot(normed2, w_gate)
    upper = dot(normed2, w_up)
    sigma = jax.nn.sigmoid(gate)
    activated = gate * sigma
    gate, upper, hidden = lax.optimization_barrier((gate, upper, (activated * upper).astype(bf)))
    sigma = jax.nn.sigmoid(gate)
    activated = gate * sigma
    grad_hidden = dot(cot_all, w_down)
    grad_gate = (grad_hidden * upper * (sigma * (1.0 + gate * (1.0 - sigma)))).astype(bf)
    grad_upper = (grad_hidden * activated).astype(bf)

    pairs_hidden = links.pair_rows(after(hidden, near_two))
    part2 = dot_trans(grad_gate, w_gate) + dot_trans(grad_upper, w_up)
    other2 = swap(part2.astype(bf))
    total_down = links.cores(product(left_cot, (after(hidden, other2), pairs_hidden)))
    grad_w_down = links.scatter(total_down)
    pairs_gate = links.pair_rows(grad_gate)

    other2 = after(other2, total_down)
    grad_normed2 = part2 + other2.astype(f32)
    grad_gain2 = jnp.sum(grad_normed2 * resid * scale2, axis=0, keepdims=True)
    grad_resid = cot_all.astype(f32) + norm_back(grad_normed2, resid, norm2_gain, scale2)
    branch = grad_resid.astype(bf)
    grad_mixed = dot(branch, w_output).astype(bf)
    grad_qk, grad_vp, grad_logit, grad_taps = mix_backward(
        item_lengths, queries, keys, values, path_raw, beta_logit, taps, solved, moved, probs, grad_mixed
    )

    def halves(array):
        return array.reshape(2, local, depth)

    left_two = near_two, links.pair_rows(after(far_two, grad_qk))
    pairs_up = links.pair_rows(grad_upper)
    near_branch, far_branch = turn(links.halving, after(branch, grad_qk))
    left_one = near_one, links.pair_rows(far_one)
    product_gate = product(left_two, (after(grad_gate, grad_qk), pairs_gate))
    total_gate = links.cores(product_gate)
    grad_w_gate = links.scatter(total_gate)
    low_logit = grad_logit.astype(bf)
    part = back(after(grad_qk, total_gate, near_branch, grad_w_down), grad_vp, (w_query, w_key, w_value, w_path))
    part = halves(part + dot_trans(low_logit, w_beta))
    part_away = pick(part, 1 - head).astype(bf)
    other1 = swap(part_away)
    part_keep = pick(part, head)
    total_up = links.cores(product(left_two, (after(grad_upper, part_away), pairs_up)))
    grad_w_up = links.scatter(total_up)
    pairs_qk = links.pair_rows(grad_qk)
    other1 = after(other1, total_up)
    grad_normed1 = part_keep + other1.astype(f32)
    inputs_own = tokens.astype(f32)
    scale_own = norm_scale(inputs_own)
    grad_tokens = pick(halves(grad_resid), head) + norm_back(grad_normed1, inputs_own, norm1_gain, scale_own)
    grad_gain1 = jnp.sum(grad_normed1 * inputs_own * scale_own, axis=0, keepdims=True)

    width = w_query.shape[1]
    low_logit, grad_gain2 = after(low_logit, total_up), after(grad_gain2, total_up)
    grad_taps = after(grad_taps, total_up)
    small = lax.dot_general(low_logit, normed1, (((0,), (0,)), ((), ())), preferred_element_type=f32)
    grad_gain1 = grad_gain1 + swap(grad_gain1)
    small = jnp.concatenate([small, grad_gain1, grad_gain2], axis=0)
    heads = w_beta.shape[1]
    rows = depth // links.count
    conv_rows = conv_kernel.shape[0] // links.count
    small = jnp.swapaxes(small.reshape(-1, links.count, rows), 0, 1)
    conv = jnp.swapaxes(grad_taps.reshape(-1, links.count, conv_rows), 0, 1).reshape(links.count, 2, rows)
    small = jnp.concatenate([small, conv], axis=1)
    small = jnp.pad(small, ((0, 0), (0, 16 - small.shape[1]), (0, DH - rows)))

    left_branch = near_branch, links.pair_rows(after(far_branch, total_up, small))
    pairs_vp = links.pair_rows(grad_vp)
    pairs_mixed = links.pair_rows(mixed, 2)
    total_qk = links.cores(product(left_one, (after(grad_qk, grad_w_gate, small), pairs_qk)))
    first_qk = links.first(total_qk)
    total_vp = links.cores(product(left_one, (after(grad_vp, grad_w_up, first_qk[0]), pairs_vp)))
    first_vp = links.first(total_vp)
    hidden_late = after(hidden, total_vp)
    part = halves(dot_trans(hidden_late, w_down))
    ffn_away = pick(part, 1 - head).astype(bf)
    ffn = swap(after(ffn_away, other1))
    resid_own = pick(halves(resid), head)
    activations = (resid_own + pick(part, head) + ffn.astype(f32)).astype(bf)
    sum_qk = links.second(first_qk)
    total_output = links.cores(product(left_branch, (after(mixed, total_vp), pairs_mixed)))
    first_output = links.first(total_output)
    sum_vp = links.second(first_vp)
    grad_w_output = links.second(first_output)
    core_small = small + links.flip(small, 1)
    pair_small = core_small + links.pair_rows(after(core_small, first_vp[0]))
    small = links.second(links.first(links.chosen(pair_small)))[:, :rows]

    width = w_query.shape[1]
    grad_w_beta = small[:heads].T
    piece = rows // 2
    gains = lax.dynamic_slice_in_dim(small[heads : heads + 2], piece * head, piece, 1)
    conv = small[heads + 2 : heads + 4].reshape(-1, heads, conv_rows)
    grad_conv = jnp.transpose(conv, (2, 1, 0))

    grad_gain1, grad_gain2 = gains[0], gains[1]
    grad_w_query, grad_w_key = sum_qk[:, :width], sum_qk[:, width:]
    grad_w_value, grad_w_path = sum_vp[:, :width], sum_vp[:, width:]
    return (
        activations,
        grad_tokens,
        grad_gain1,
        grad_w_query,
        grad_w_key,
        grad_w_value,
        grad_w_path,
        grad_w_beta,
        grad_conv,
        grad_w_output,
        grad_gain2,
        grad_w_gate,
        grad_w_up,
        grad_w_down,
    )


def solution(mesh):
    in_specs = (
        P(("dp", "head"), None),
        P(),
        P(None, "head"),
        P(None, "head"),
        P(None, "head"),
        P(None, "head"),
        P(None, "head"),
        P(None, "head", None),
        P(None, "head"),
        P(),
        P(None, "head"),
        P(None, "head"),
        P(None, "head"),
        P("dp"),
        P(("dp", "head"), None),
    )
    out_specs = (
        P(("dp", "head"), None),
        P(("dp", "head"), None),
        P(("dp", "head")),
        P("dp", "head"),
        P("dp", "head"),
        P("dp", "head"),
        P("dp", "head"),
        P("dp", "head"),
        P("dp", "head", None),
        P("dp", "head"),
        P(("dp", "head")),
        P("dp", "head"),
        P("dp", "head"),
        P("dp", "head"),
    )
    return jax.shard_map(
        per_device, mesh=mesh, in_specs=in_specs, out_specs=out_specs, check_vma=False
    )
```
